256 devices in a mesh: row: 16 (over y, x_hi, core), col: 16 (over z, x_lo).
Axes of the slice: x: 4 (x_hi: 2, x_lo: 2; x = x_hi * 2 + x_lo), y: 4, z: 8, core: 2. Of those that a mesh axis runs over, the one named last changes fastest.
Arguments:
- queries: bfloat16 [8192, 2048], P('row'), may hold values from -6 to 6
- keys: bfloat16 [4096, 2048], P('col'), may hold values from -6 to 6
- values: bfloat16 [4096, 2048], P('col'), may hold values from -6 to 6
- out_grad: bfloat16 [8192, 2048], P('row'), may hold values from -6 to 6
- tau: float32 [16, 8192], P(None, 'row'), may hold values from 2 to 3.5
- alpha: float32 [16], replicated, may hold values from 1.25 to 1.75
- query_blocks: int32 [64], P('row'), may hold values from 0 to 31
- key_blocks: int32 [32], P('col'), may hold values from 0 to 31, each once
Outputs:
- query_grad: bfloat16 [2048, 8192], P('col', 'row')
- key_grad: bfloat16 [2048, 4096], P('row', 'col')
- value_grad: bfloat16 [2048, 4096], P('row', 'col')
The draws below stay inside these ranges and needn't reach their ends.
All inputs are finite; a program needn't handle non-finite values.
Results may differ from the reference program's by a relative error of at most 0.007.
Values may be sent and summed in bfloat16 or wider, within the bound.
A program may use at most 128 MiB of HBM per device.

```python
import math
import jax
import jax.numpy as jnp
from jax import lax

H = 16
DH = 128
D = 2048
BLK = 128
QUERIES = 8192
KEYS = 4096


def plant(array, key, least, high):
    shape = array.shape
    spot = [jax.random.randint(jax.random.fold_in(key, axis), (), 0, shape[axis]) for axis in range(len(shape))]
    array = array.at[tuple(spot)].set(least)
    longest = shape.index(max(shape))
    spot[longest] = (spot[longest] + 1) % shape[longest]
    return array.at[tuple(spot)].set(high)


def block_scale(stream_key, extent, pieces, low, top_value):
    def one(dim, blocks):
        draws = jax.random.uniform(jax.random.fold_in(jax.random.fold_in(stream_key, 6), dim), (blocks,), jnp.float32, low / len(pieces), top_value / len(pieces))
        return jnp.repeat(jnp.exp(draws), extent[dim] // blocks).reshape((-1,) + (1,) * (len(extent) - dim - 1))

    loudness = one(*pieces[0])
    for cut in pieces[1:]:
        loudness = loudness * one(*cut)
    return loudness


def noise(rng, extent, width, most, pieces=(), kind=jnp.bfloat16):
    values = jax.random.normal(rng, extent, jnp.float32) * width
    if len(pieces) > 0:
        values = block_scale(rng, extent, pieces, -0.22, 0.18) * values
    return jnp.clip(values, min=-most, max=most).astype(kind)


def setup_inputs(seed: int = 0) -> dict:
    splits = jax.random.split(jax.random.key(seed), 9)
    queries = noise(splits[0], (QUERIES, D), 1.0, 6.0, ((0, 16),))
    keys = noise(splits[1], (KEYS, D), 1.0, 6.0, ((0, 16),))
    values = noise(splits[2], (KEYS, D), 1.0, 6.0, ((0, 16),))
    out_grad = noise(splits[3], (QUERIES, D), 1.0, 6.0, ((0, 16),))
    tau = jnp.clip(2.0 + 1.5 * jax.random.uniform(splits[4], (H, QUERIES), jnp.float32) ** block_scale(splits[4], (H, QUERIES), ((1, 16),), -0.2, 0.2), 2.0, 3.5)
    alpha = jnp.clip(jax.random.uniform(splits[5], (H,), jnp.float32, 1.25, 1.75), 1.25, 1.75)
    query_blocks = plant(jax.random.randint(splits[6], (QUERIES // BLK,), 0, KEYS // BLK), jax.random.fold_in(splits[6], 1), 0, (KEYS // BLK) - 1).astype(jnp.int32)
    key_blocks = jax.random.permutation(splits[7], KEYS // BLK).astype(jnp.int32)
    return dict(queries=queries, keys=keys, values=values, out_grad=out_grad, tau=tau, alpha=alpha, query_blocks=query_blocks, key_blocks=key_blocks)


def block_positions(blocks, block_size):
    within = jnp.arange(block_size, dtype=jnp.int32)
    return (blocks[:, None] * block_size + within[None, :]).reshape(-1)

def reference(queries, keys, values, out_grad, tau, alpha, query_blocks, key_blocks):
    factor = 1.0 / math.sqrt(DH)
    allowed = block_positions(key_blocks, BLK)[None, :] <= block_positions(query_blocks, BLK)[:, None]

    def head_grads(head):
        query_head = lax.dynamic_slice_in_dim(queries, head * DH, DH, 1)
        key_head = lax.dynamic_slice_in_dim(keys, head * DH, DH, 1)
        value_head = lax.dynamic_slice_in_dim(values, head * DH, DH, 1)
        grad_head = lax.dynamic_slice_in_dim(out_grad, head * DH, DH, 1)
        excess = alpha[head] - 1.0
        scores = jnp.dot(query_head, key_head.T, preferred_element_type=jnp.float32) * factor
        support = jnp.where(allowed, jnp.maximum(excess * (scores - tau[head][:, None]), 0.0), 0.0)
        probabilities = (support ** (1.0 / excess)).astype(jnp.bfloat16)
        weights = support ** ((1.0 - excess) / excess)
        prob_grad = jnp.dot(grad_head, value_head.T, preferred_element_type=jnp.float32)
        totals = lax.optimization_barrier(jnp.sum(weights * prob_grad, axis=1))
        masses = lax.optimization_barrier(jnp.sum(weights, axis=1))
        row_shift = totals / jnp.maximum(masses, 1.0)
        score_grad = (weights * (prob_grad - row_shift[:, None])).astype(jnp.bfloat16)
        query_part = factor * jnp.dot(score_grad, key_head, preferred_element_type=jnp.float32)
        key_part = factor * jnp.dot(score_grad.T, query_head, preferred_element_type=jnp.float32)
        value_part = jnp.dot(probabilities.T, grad_head, preferred_element_type=jnp.float32)
        return (query_part.T, key_part.T, value_part.T)
    query_parts, key_parts, value_parts = lax.map(head_grads, jnp.arange(H, dtype=jnp.int32))
    return (query_parts.reshape(H * DH, QUERIES).astype(jnp.bfloat16), key_parts.reshape(H * DH, KEYS).astype(jnp.bfloat16), value_parts.reshape(H * DH, KEYS).astype(jnp.bfloat16))
```

```python
import math

import jax
import jax.numpy as jnp
from jax import lax
from jax.experimental import pallas as pl
from jax.experimental.pallas import tpu as pltpu
from jax.sharding import PartitionSpec as P

MESH = pl.DeviceIdType.MESH
DH = 128
BLK = 128
QN = 512
N = 16
SH = 32
F32 = jnp.float32
BF16 = jnp.bfloat16
FACTOR = 1.0 / math.sqrt(DH)


def dot(a, b):
    return jnp.dot(a, b, preferred_element_type=F32)


def kernel(
    queries, keys, values, out_grad, tau, alpha, query_blocks, key_blocks,
    dq_out, dk_out, dv_out,
    kbuf, vbuf, qh, gh, tau_v, send_k, send_v, blk_s,
    gk, gv, blk,
    qt, gt, w_all, dp_all, probs, tot, mass, dq_acc,
    pk, pv, core_k, core_v, sum_k, sum_v, half_k, half_v, full_k, full_v,
    own_k, own_v, col_k, col_v, row_k, row_v,
    in_sem, a_send, a_recv, y_send, y_recv, m_send, m_recv, c_send, c_recv,
    h_send, h_recv, f_send, f_recv, p_send, p_recv, q_send, q_recv,
):
    r = lax.axis_index("row")
    c = lax.axis_index("col")
    y = r // 4
    xh = (r // 2) % 2
    core = r % 2
    other = 1 - core
    mate = y * 4 + xh * 2 + other
    yp = (y + 1) % 4
    ym = (y + 3) % 4
    yo = (y + 2) % 4
    row_p = yp * 4 + xh * 2 + core
    row_m = ym * 4 + xh * 2 + core
    share = y * 2 + core

    def send(src, dst, ssem, rsem, row, col):
        return pltpu.make_async_remote_copy(
            src_ref=src, dst_ref=dst, send_sem=ssem, recv_sem=rsem,
            device_id=(row, col), device_id_type=MESH,
        )

    loads = [
        pltpu.make_async_copy(keys.at[pl.ds(pl.multiple_of(share * SH, SH), SH), :], kbuf, in_sem.at[0]),
        pltpu.make_async_copy(values.at[pl.ds(pl.multiple_of(share * SH, SH), SH), :], vbuf, in_sem.at[1]),
        pltpu.make_async_copy(queries.at[:, pl.ds(pl.multiple_of(c * DH, DH), DH)], qh, in_sem.at[2]),
        pltpu.make_async_copy(out_grad.at[:, pl.ds(pl.multiple_of(c * DH, DH), DH)], gh, in_sem.at[3]),
        pltpu.make_async_copy(tau, tau_v, in_sem.at[4]),
    ]
    for load in loads:
        load.start()
    barrier = pltpu.get_barrier_semaphore()
    for j in range(1, N):
        pl.semaphore_signal(barrier, inc=1, device_id=(r, (c + j) % N), device_id_type=MESH)
        pl.semaphore_signal(barrier, inc=1, device_id=((r + j) % N, c), device_id_type=MESH)
    kb = [jnp.full((8, DH), key_blocks[i]).astype(F32) for i in range(2)]
    blk_s[...] = jnp.concatenate(kb, axis=0).astype(BF16)
    loads[0].wait()
    for h in range(N):
        send_k[h] = kbuf[:, h * DH : (h + 1) * DH]
    loads[1].wait()
    for h in range(N):
        send_v[h] = vbuf[:, h * DH : (h + 1) * DH]
    pl.semaphore_wait(barrier, 2 * (N - 1))

    def to_col(j):
        peer = (c + j) % N
        return [
            send(send_k.at[peer], gk.at[share, c], a_send.at[0, j], a_recv.at[0, c], r, peer),
            send(blk_s, blk.at[c], a_send.at[1, j], a_recv.at[1, c], r, peer),
            send(send_v.at[peer], gv.at[share, c], a_send.at[2, j], a_recv.at[2, c], r, peer),
        ]

    def from_col(j):
        peer = (c + j) % N
        return [
            send(send_k.at[c], gk.at[share, peer], a_send.at[0, j], a_recv.at[0, peer], r, peer),
            send(blk_s, blk.at[peer], a_send.at[1, j], a_recv.at[1, peer], r, peer),
            send(send_v.at[c], gv.at[share, peer], a_send.at[2, j], a_recv.at[2, peer], r, peer),
        ]

    sent = [to_col(j) for j in range(1, N)]
    for kind in (0, 1, 2):
        for copies in sent:
            copies[kind].start()
    gk[share, c] = send_k[c]
    gv[share, c] = send_v[c]
    blk[c] = blk_s[...]

    for load in loads[2:]:
        load.wait()
    qt[...] = qh[...].T
    gt[...] = gh[...].T
    tot[...] = jnp.zeros_like(tot)
    mass[...] = jnp.zeros_like(mass)
    dq_acc[...] = jnp.zeros_like(dq_acc)
    excess = jnp.full((8, QN), alpha[c]) - 1.0
    scale = excess * FACTOR
    shift_in = jnp.broadcast_to(tau_v[pl.ds(c, 1), :], (8, QN)) * excess
    power = (1.0 - excess) / excess * (1.0 / math.log(2.0))
    lane = lax.broadcasted_iota(jnp.int32, (8, QN), 1)
    qpos = lane % BLK
    for i in range(4):
        qpos = qpos + jnp.where(lane // BLK == i, query_blocks[i] * BLK, 0)
    qpos = qpos.astype(F32)
    bound = [qpos - (lax.broadcasted_iota(jnp.int32, (8, QN), 0) + 8 * i).astype(F32) for i in range(SH // 8)]

    for j in range(1, N):
        came = from_col(j)
        came[0].wait_recv()
        came[1].wait_recv()

    def gather_copies(kind, buf):
        mine = buf.at[share]
        share_p = yp * 2 + core
        share_m = ym * 2 + core
        first = buf.at[share_p, 0 : N // 2]
        second = buf.at[share_m, N // 2 : N]
        far = yo * 2 + core
        out = dict(
            p=send(mine, mine, y_send.at[kind, 0], y_recv.at[kind, 0], row_p, c),
            m=send(mine, mine, y_send.at[kind, 1], y_recv.at[kind, 1], row_m, c),
            fm=send(first, first, y_send.at[kind, 2], y_recv.at[kind, 2], row_m, c),
            fp=send(second, second, y_send.at[kind, 3], y_recv.at[kind, 3], row_p, c),
        )
        for t, s in enumerate((share, share_p, share_m, far)):
            out["mate", t] = send(buf.at[s], buf.at[s], m_send.at[kind, t], m_recv.at[kind, t], mate, c)
        got = dict(
            p=send(buf.at[share_m], buf.at[share_m], y_send.at[kind, 0], y_recv.at[kind, 0], row_m, c),
            m=send(buf.at[share_p], buf.at[share_p], y_send.at[kind, 1], y_recv.at[kind, 1], row_p, c),
            fm=send(buf.at[far, 0 : N // 2], buf.at[far, 0 : N // 2], y_send.at[kind, 2], y_recv.at[kind, 2], row_p, c),
            fp=send(buf.at[far, N // 2 : N], buf.at[far, N // 2 : N], y_send.at[kind, 3], y_recv.at[kind, 3], row_m, c),
        )
        for t, yy in enumerate((y, yp, ym, yo)):
            s = yy * 2 + other
            got["mate", t] = send(buf.at[s], buf.at[s], m_send.at[kind, t], m_recv.at[kind, t], mate, c)
        return out, got

    k_out, k_got = gather_copies(0, gk)
    v_out, v_got = gather_copies(1, gv)
    for key in ("p", "m", ("mate", 0)):
        k_out[key].start()
    for j in range(1, N):
        from_col(j)[2].wait_recv()
    for key in ("p", "m", ("mate", 0)):
        v_out[key].start()

    def first_pass(s):
        k_s = gk[s].reshape(N * SH, DH)
        v_s = gv[s].reshape(N * SH, DH)
        scores = dot(k_s, qt[...])
        dp = dot(v_s, gt[...])
        dp_all[s] = dp
        within = ((s % 4) * SH).astype(F32)
        late = s // 4
        t_sum = jnp.zeros((8, QN), F32)
        m_sum = jnp.zeros((8, QN), F32)
        for j in range(N):
            b16 = blk[j].astype(F32)
            b = jnp.where(late == 0, b16[0:8], b16[8:16]) * BLK + within
            b = jnp.concatenate([b] * (QN // BLK), axis=1)
            for i in range(SH // 8):
                lo = j * SH + i * 8
                x = scores[lo : lo + 8] * scale - shift_in
                x = jnp.where(b <= bound[i], jnp.maximum(x, 0.0), 0.0)
                w = jnp.exp2(jnp.log(x) * power)
                w_all[s, lo : lo + 8, :] = w
                probs[lo : lo + 8, :] = w * x
                t_sum = t_sum + w * dp[lo : lo + 8]
                m_sum = m_sum + w
        tot[...] += t_sum
        mass[...] += m_sum
        pv[s] = dot(probs[...].astype(BF16), gh[...]).astype(BF16).reshape(N, SH, DH)

    def core_copy(kind, part, arrived, yy):
        s = yy * 2 + other
        return send(part.at[s], arrived.at[yy], c_send.at[kind, yy], c_recv.at[kind, yy], mate, c)

    def pass_one(i, carry):
        t = i // 2

        @pl.when(i == 1)
        def _():
            k_got["mate", 0].wait_recv()
            v_got["mate", 0].wait_recv()

        @pl.when(i == 2)
        def _():
            for got, out in ((k_got, k_out), (v_got, v_out)):
                got["m"].wait_recv()
                out["fm"].start()
                out["mate", 1].start()
                got["p"].wait_recv()
                out["fp"].start()
                out["mate", 2].start()

        @pl.when(i == 3)
        def _():
            k_got["mate", 1].wait_recv()
            v_got["mate", 1].wait_recv()

        @pl.when(i == 5)
        def _():
            k_got["mate", 2].wait_recv()
            v_got["mate", 2].wait_recv()

        @pl.when(i == 6)
        def _():
            for got, out in ((k_got, k_out), (v_got, v_out)):
                got["fm"].wait_recv()
                got["fp"].wait_recv()
                out["mate", 3].start()

        @pl.when(i == 7)
        def _():
            k_got["mate", 3].wait_recv()
            v_got["mate", 3].wait_recv()

        yy = (y + t + t // 2 - 2 * (t // 3)) % 4
        half = i % 2
        s = yy * 2 + core + half * (other - core)
        first_pass(s)

        @pl.when(half == 1)
        def _():
            core_copy(1, pv, core_v, yy).start()

        return carry

    lax.fori_loop(0, 8, pass_one, 0)

    def add_core(kind, part, arrived, total, yy):
        core_copy(kind, part, arrived, yy).wait_recv()
        total[yy] = (part[yy * 2 + core].astype(F32) + arrived[yy].astype(F32)).astype(BF16)

    H2 = N // 2

    def half_copies(kind, total, arrived):
        return (
            send(total.at[yo, 0:H2], arrived.at[0], h_send.at[kind, 0], h_recv.at[kind, 0], row_p, c),
            send(total.at[yo, H2:N], arrived.at[1], h_send.at[kind, 1], h_recv.at[kind, 1], row_m, c),
        )

    def full_copies(kind, total, arrived):
        return (
            send(total.at[yp], arrived.at[0], f_send.at[kind, 0], f_recv.at[kind, 0], row_p, c),
            send(total.at[ym], arrived.at[1], f_send.at[kind, 1], f_recv.at[kind, 1], row_m, c),
        )

    def add_half_p(kind, total, arrived):
        half_copies(kind, total, arrived)[0].wait_recv()
        total[yp, 0:H2] = (total[yp, 0:H2].astype(F32) + arrived[0].astype(F32)).astype(BF16)
        full_copies(kind, total, full_k if kind == 0 else full_v)[0].start()

    def add_half_m(kind, total, arrived):
        half_copies(kind, total, arrived)[1].wait_recv()
        total[ym, H2:N] = (total[ym, H2:N].astype(F32) + arrived[1].astype(F32)).astype(BF16)
        full_copies(kind, total, full_k if kind == 0 else full_v)[1].start()

    def col_copy(kind, j, out):
        peer = (c + j) % N
        src, dst = (own_k, col_k) if kind == 0 else (own_v, col_v)
        if out:
            return send(src.at[peer], dst.at[c], p_send.at[kind, j], p_recv.at[kind, c], r, peer)
        return send(src.at[c], dst.at[peer], p_send.at[kind, j], p_recv.at[kind, peer], r, peer)

    def row_copy(kind, j, out):
        peer = (r + j) % N
        src, dst = (col_k, row_k) if kind == 0 else (col_v, row_v)
        if out:
            return send(src.at[peer], dst.at[r], q_send.at[kind, j], q_recv.at[kind, r], peer, c)
        return send(src.at[r], dst.at[peer], q_send.at[kind, j], q_recv.at[kind, peer], peer, c)

    def add_own(kind, total, arrived, own, landed):
        for copy in full_copies(kind, total, arrived):
            copy.wait_recv()
        own[...] = (total[y].astype(F32) + arrived[0].astype(F32) + arrived[1].astype(F32)).astype(BF16)
        for j in range(1, N):
            col_copy(kind, j, True).start()
        landed[c] = own[c]

    def to_rows(kind, landed, final):
        for j in range(1, N):
            col_copy(kind, j, False).wait_recv()
        for j in range(1, N):
            row_copy(kind, j, True).start()
        final[r] = landed[r]

    def finish(kind, final, out, factor):
        for j in range(1, N):
            row_copy(kind, j, False).wait_recv()
        both = final[...].astype(F32).reshape(4, 2, 2, SH, DH)
        both = (both[:, 0] + both[:, 1]).reshape(8 * SH, DH)
        out[...] = (both.T * factor).astype(BF16)

    total_all = jnp.sum(tot[...], axis=0, keepdims=True)
    mass_all = jnp.sum(mass[...], axis=0, keepdims=True)
    row_shift = jnp.broadcast_to(total_all / jnp.maximum(mass_all, 1.0), (8, QN))

    add_core(1, pv, core_v, sum_v, yo)
    for copy in half_copies(1, sum_v, half_v):
        copy.start()
    add_core(1, pv, core_v, sum_v, yp)
    add_core(1, pv, core_v, sum_v, ym)
    add_core(1, pv, core_v, sum_v, y)

    def second_pass(s):
        for j in range(N * SH // 8):
            lo = j * 8
            probs[lo : lo + 8, :] = w_all[s, lo : lo + 8, :] * (dp_all[s, lo : lo + 8, :] - row_shift)
        ds = probs[...].astype(BF16)
        pk[s] = dot(ds, qh[...]).astype(BF16).reshape(N, SH, DH)
        dq_acc[...] += lax.dot_general(
            gk[s].reshape(N * SH, DH), ds, (((0,), (0,)), ((), ())), preferred_element_type=F32
        )

    def pass_two(i, carry):
        t = 3 - i // 2
        yy = (y + t + t // 2 - 2 * (t // 3)) % 4
        half = i % 2
        s = yy * 2 + other + half * (core - other)
        second_pass(s)

        @pl.when(half == 0)
        def _():
            core_copy(0, pk, core_k, yy).start()

        @pl.when(half == 1)
        def _():
            add_core(0, pk, core_k, sum_k, yy)

        @pl.when(i == 1)
        def _():
            for copy in half_copies(0, sum_k, half_k):
                copy.start()
            add_half_p(1, sum_v, half_v)
            add_half_m(1, sum_v, half_v)

        @pl.when(i == 3)
        def _():
            add_half_m(0, sum_k, half_k)

        @pl.when(i == 5)
        def _():
            add_half_p(0, sum_k, half_k)
            add_own(1, sum_v, full_v, own_v, col_v)

        return carry

    lax.fori_loop(0, 8, pass_two, 0)
    add_own(0, sum_k, full_k, own_k, col_k)
    to_rows(1, col_v, row_v)
    dq_out[...] = (dq_acc[...] * FACTOR).astype(BF16)
    to_rows(0, col_k, row_k)
    finish(1, row_v, dv_out, 1.0)
    finish(0, row_k, dk_out, FACTOR)

    for copies in sent:
        for copy in copies:
            copy.wait_send()
    for out in (k_out, v_out):
        for copy in out.values():
            copy.wait_send()
    for kind, part, arrived, total, halves, fulls in (
        (0, pk, core_k, sum_k, half_k, full_k),
        (1, pv, core_v, sum_v, half_v, full_v),
    ):
        for yy in range(4):
            core_copy(kind, part, arrived, yy).wait_send()
        for copy in half_copies(kind, total, halves) + full_copies(kind, total, fulls):
            copy.wait_send()
        for j in range(1, N):
            col_copy(kind, j, True).wait_send()
            row_copy(kind, j, True).wait_send()


def local(queries, keys, values, out_grad, tau, alpha, query_blocks, key_blocks):
    any_ = pl.BlockSpec(memory_space=pl.ANY)
    smem = pl.BlockSpec(memory_space=pltpu.SMEM)
    vmem = pl.BlockSpec(memory_space=pltpu.VMEM)
    V = pltpu.VMEM
    dma = pltpu.SemaphoreType.DMA
    part = (8, N, SH, DH)
    quarter = (4, N, SH, DH)
    return pl.pallas_call(
        kernel,
        out_shape=(
            jax.ShapeDtypeStruct((DH, QN), BF16),
            jax.ShapeDtypeStruct((DH, 2 * BLK), BF16),
            jax.ShapeDtypeStruct((DH, 2 * BLK), BF16),
        ),
        in_specs=[any_] * 5 + [smem] * 3,
        out_specs=(vmem,) * 3,
        scratch_shapes=[
            V((SH, N * DH), BF16), V((SH, N * DH), BF16), V((QN, DH), BF16), V((QN, DH), BF16), V((N, QN), F32),
            V((N, SH, DH), BF16), V((N, SH, DH), BF16), V((16, DH), BF16),
            V(part, BF16), V(part, BF16), V((N, 16, DH), BF16),
            V((DH, QN), BF16), V((DH, QN), BF16), V((8, N * SH, QN), F32), V((8, N * SH, QN), F32), V((N * SH, QN), F32),
            V((8, QN), F32), V((8, QN), F32), V((DH, QN), F32),
            V(part, BF16), V(part, BF16), V(quarter, BF16), V(quarter, BF16), V(quarter, BF16), V(quarter, BF16),
            V((2, N // 2, SH, DH), BF16), V((2, N // 2, SH, DH), BF16), V((2, N, SH, DH), BF16), V((2, N, SH, DH), BF16),
            V((N, SH, DH), BF16), V((N, SH, DH), BF16), V((N, SH, DH), BF16), V((N, SH, DH), BF16), V((N, SH, DH), BF16), V((N, SH, DH), BF16),
            dma((5,)), dma((3, N)), dma((3, N)), dma((2, 4)), dma((2, 4)), dma((2, 4)), dma((2, 4)), dma((2, 4)), dma((2, 4)),
            dma((2, 2)), dma((2, 2)), dma((2, 2)), dma((2, 2)), dma((2, N)), dma((2, N)), dma((2, N)), dma((2, N)),
        ],
        compiler_params=pltpu.CompilerParams(
            collective_id=0, has_side_effects=True, vmem_limit_bytes=48 * 1024 * 1024
        ),
    )(queries, keys, values, out_grad, tau, alpha, query_blocks, key_blocks)


def solution(mesh):
    in_specs = (
        P("row", None), P("col", None), P("col", None), P("row", None),
        P(None, "row"), P(), P("row"), P("col"),
    )
    out_specs = (P("col", "row"), P("row", "col"), P("row", "col"))
    return jax.shard_map(local, mesh=mesh, in_specs=in_specs, out_specs=out_specs, check_vma=False)
```

```python
import math

import jax
import jax.numpy as jnp
from jax import lax
from jax.experimental import pallas as pl
from jax.experimental.pallas import tpu as pltpu
from jax.sharding import PartitionSpec as P

MESH = pl.DeviceIdType.MESH
DH = 128
BLK = 128
QN = 512
N = 16
SH = 32
KN = N * SH
M = 8
F32 = jnp.float32
BF16 = jnp.bfloat16
FACTOR = 1.0 / math.sqrt(DH)


def dot(a, b):
    return jnp.dot(a, b, preferred_element_type=F32)


def dot_nt(a, b):
    return lax.dot_general(a, b, (((1,), (1,)), ((), ())), preferred_element_type=F32)


def place(t):
    return t + t // 2 - 2 * (t // 3)


def kernel(
    queries, keys, values, out_grad, tau_in, alpha_in, query_blocks_in, key_blocks_in,
    dq_out, dk_out, dv_out,
    alpha, query_blocks, key_blocks, tau,
    gk, gv, gb, gb_send,
    gq, gg, info,
    kt, w_all, dp_all, probs, dv_acc, dk_acc, stats, stats_in, shifts,
    dq_mine, dq_mate_out, dq_mate_in, dq_sum, dq_in, own_k, own_v, row_k, row_v,
    in_sem, a_send, a_recv, y_send, y_recv, m_send, m_recv, i_send, i_recv, s_send, s_recv,
    c_send, c_recv, d_send, d_recv, p_send, p_recv,
):
    r = lax.axis_index("row")
    c = lax.axis_index("col")
    y = r // 4
    xh = (r // 2) % 2
    core = r % 2
    other = 1 - core
    share = y * 2 + core

    def row_of(yy, cc):
        return yy * 4 + xh * 2 + cc

    mate = row_of(y, other)

    def send(src, dst, ssem, rsem, row, col):
        return pltpu.make_async_remote_copy(
            src_ref=src, dst_ref=dst, send_sem=ssem, recv_sem=rsem,
            device_id=(row, col), device_id_type=MESH,
        )

    def member(j):
        yy = (y + j // 2) % 4
        cc = (core + j) % 2
        return yy, cc, yy * 2 + cc

    barrier = pltpu.get_barrier_semaphore()

    def greet(row, col):
        pl.semaphore_signal(barrier, inc=1, device_id=(row, col), device_id_type=MESH)

    for j in range(1, N):
        greet(r, (c + j) % N)
    for j in range(1, M):
        yy, cc, _ = member(j)
        greet(row_of(yy, cc), c)
    for j in range(1, N):
        greet((r + j) % N, r)

    @pl.when(c != r)
    def _():
        greet(r, r)

    key_rows = pl.ds(pl.multiple_of(share * SH, SH), SH)

    def head(h):
        return pl.ds(pl.multiple_of(h * DH, DH), DH)

    loads = [
        pltpu.make_async_copy(key_blocks_in, key_blocks, in_sem.at[0]),
        pltpu.make_async_copy(query_blocks_in, query_blocks, in_sem.at[1]),
        pltpu.make_async_copy(alpha_in, alpha, in_sem.at[2]),
        pltpu.make_async_copy(tau_in, tau, in_sem.at[3]),
        pltpu.make_async_copy(queries.at[:, head(c)], gq.at[share], in_sem.at[4]),
        pltpu.make_async_copy(out_grad.at[:, head(c)], gg.at[share], in_sem.at[5]),
        pltpu.make_async_copy(keys.at[key_rows, head(c)], gk.at[c], in_sem.at[6]),
        pltpu.make_async_copy(values.at[key_rows, head(c)], gv.at[c], in_sem.at[7]),
    ]
    for load in loads:
        load.start()
    for load in loads[:4]:
        load.wait()
    base = (key_blocks[share // 4] * BLK + (share % 4) * SH).astype(F32)
    gb_send[...] = jnp.full((8, DH), base)
    gb[c] = gb_send[...]
    line = tau[pl.ds(c, 1), :]
    for i in range(4):
        info[share, i : i + 1, :] = line[:, i * DH : (i + 1) * DH]
        info[share, 4 + i : 5 + i, :] = jnp.full((1, DH), query_blocks[i] * BLK).astype(F32)
    for load in loads[4:6]:
        load.wait()

    apart = ((c + N - r) % N + N - 1) // N
    pl.semaphore_wait(barrier, (N - 1) + (M - 1) + (N - 1) + apart)

    def y_copy(kind, buf, t, out):
        step = (1, 3, 2)[t - 1]
        to = row_of((y + step) % 4, core)
        frm_y = (y + 4 - step) % 4
        frm = frm_y * 2 + core
        if out:
            return send(buf.at[share], buf.at[share], y_send.at[kind, t - 1], y_recv.at[kind, t - 1], to, c)
        return send(buf.at[frm], buf.at[frm], y_send.at[kind, t - 1], y_recv.at[kind, t - 1], row_of(frm_y, core), c)

    def mate_copy(kind, buf, t, out):
        yy = (y + 4 - (0, 1, 3, 2)[t]) % 4
        m = yy * 2 + (core if out else other)
        return send(buf.at[m], buf.at[m], m_send.at[kind, t], m_recv.at[kind, t], mate, c)

    both = ((0, gq), (1, gg))
    for t in (1, 2):
        for kind, buf in both:
            y_copy(kind, buf, t, True).start()

    def col_copy(kind, j, out):
        peer = (c + j) % N
        frm = c if out else peer
        src, dst = (
            (keys.at[key_rows, head(peer)], gk.at[frm]),
            (values.at[key_rows, head(peer)], gv.at[frm]),
            (gb_send, gb.at[frm]),
        )[kind]
        return send(src, dst, a_send.at[kind, j], a_recv.at[kind, frm], r, peer)

    far_first = sorted(range(1, N), key=lambda j: -min(j, N - j))
    for kind in (0, 1):
        for j in far_first:
            col_copy(kind, j, True).start()
    for kind, buf in both:
        y_copy(kind, buf, 3, True).start()
    for kind, buf in both:
        mate_copy(kind, buf, 0, True).start()
    for j in far_first:
        col_copy(2, j, True).start()

    def info_copy(j, out):
        yy, cc, m = member(j)
        frm = share if out else m
        return send(info.at[frm], info.at[frm], i_send.at[m], i_recv.at[frm], row_of(yy, cc), c)

    for j in range(1, M):
        info_copy(j, True).start()

    dv_acc[...] = jnp.zeros_like(dv_acc)
    dk_acc[...] = jnp.zeros_like(dk_acc)
    excess = jnp.full((8, QN), alpha[c]) - 1.0
    scale = excess * FACTOR
    power = (1.0 - excess) / excess * (1.0 / math.log(2.0))
    lane = lax.broadcasted_iota(jnp.int32, (8, QN), 1) % BLK
    row8 = lax.broadcasted_iota(jnp.int32, (8, QN), 0)
    ahead = (lane - row8).astype(F32)

    def wide(tile, lo):
        line = jnp.concatenate([tile[lo + i : lo + i + 1, :] for i in range(4)], axis=1)
        return jnp.broadcast_to(line, (8, QN))

    for t in (1, 2):
        for kind, buf in both:
            y_copy(kind, buf, t, False).wait_recv()
            mate_copy(kind, buf, t, True).start()
    for j in range(1, M):
        info_copy(j, False).wait_recv()
    for load in loads[6:]:
        load.wait()
    for kind in (0, 1, 2):
        for j in far_first:
            col_copy(kind, j, False).wait_recv()
    kt[...] = gk[...].reshape(KN, DH).T

    def first_pass(m, place_in_order):
        scores = dot_nt(gk[...].reshape(KN, DH), gq[m])
        dp = dot_nt(gv[...].reshape(KN, DH), gg[m])
        dp_all[m] = dp
        tile = info[m]
        shift_in = wide(tile, 0) * excess
        query = wide(tile, 4) + ahead
        t_sum = jnp.zeros((8, QN), F32)
        m_sum = jnp.zeros((8, QN), F32)
        for j in range(N):
            b = jnp.concatenate([gb[j]] * (QN // DH), axis=1)
            for i in range(SH // 8):
                lo = j * SH + i * 8
                x = scores[lo : lo + 8] * scale - shift_in
                x = jnp.where(b + 8.0 * i <= query, jnp.maximum(x, 0.0), 0.0)
                w = jnp.exp2(jnp.log(x) * power)
                w_all[m, lo : lo + 8, :] = w
                probs[lo : lo + 8, :] = w * x
                t_sum = t_sum + w * dp[lo : lo + 8]
                m_sum = m_sum + w
        dv_acc[...] += dot(probs[...].astype(BF16), gg[m])
        t_sum = jnp.sum(t_sum, axis=0, keepdims=True)
        m_sum = jnp.sum(m_sum, axis=0, keepdims=True)
        parts = [s[:, i * DH : (i + 1) * DH] for s in (t_sum, m_sum) for i in range(4)]
        stats[place_in_order] = jnp.concatenate(parts, axis=0)

    BATCH = ((0, 6), (6, 8))

    def stats_copy(batch, j, out):
        yy, cc, m = member(j)
        frm = share if out else m
        lo, hi = BATCH[batch]
        return send(
            stats.at[lo:hi], stats_in.at[frm, lo:hi], s_send.at[batch, m], s_recv.at[batch, frm], row_of(yy, cc), c
        )

    def pass_one(i, carry):
        @pl.when(i == 1)
        def _():
            for kind, buf in both:
                mate_copy(kind, buf, 0, False).wait_recv()

        @pl.when(i == 3)
        def _():
            for kind, buf in both:
                mate_copy(kind, buf, 1, False).wait_recv()

        @pl.when(i == 4)
        def _():
            for kind, buf in both:
                y_copy(kind, buf, 3, False).wait_recv()
                mate_copy(kind, buf, 3, True).start()

        @pl.when(i == 5)
        def _():
            for kind, buf in both:
                mate_copy(kind, buf, 2, False).wait_recv()

        @pl.when(i == 7)
        def _():
            for kind, buf in both:
                mate_copy(kind, buf, 3, False).wait_recv()

        yy = (y + 4 - place(i // 2)) % 4
        first_pass(yy * 2 + (core + i) % 2, i)

        @pl.when(i == 5)
        def _():
            for j in range(1, M):
                stats_copy(0, j, True).start()

        return carry

    lax.fori_loop(0, M, pass_one, 0)
    for j in range(1, M):
        stats_copy(1, j, True).start()

    def last_copy(kind, j, out):
        src, dst = ((own_k, row_k), (own_v, row_v))[kind]
        if out:
            peer = (c + j) % N
            return send(src.at[peer], dst.at[r], p_send.at[kind, j], p_recv.at[kind, r], c, peer)
        peer = (r + j) % N
        return send(src.at[c], dst.at[peer], p_send.at[kind, j], p_recv.at[kind, peer], peer, r)

    def send_last(kind, total):
        src, dst = ((own_k, row_k), (own_v, row_v))[kind]
        src[...] = total.astype(BF16).reshape(N, SH, DH)
        for j in range(1, N):
            last_copy(kind, j, True).start()

        @pl.when(c != r)
        def _():
            last_copy(kind, 0, True).start()

        @pl.when(c == r)
        def _():
            dst[r] = src[c]

    def finish(kind, out, factor):
        for j in range(1, N):
            last_copy(kind, j, False).wait_recv()

        @pl.when(c != r)
        def _():
            last_copy(kind, 0, False).wait_recv()

        final = (row_k, row_v)[kind]
        pairs = final[...].astype(F32).reshape(4, 2, 2, SH, DH)
        pairs = (pairs[:, 0] + pairs[:, 1]).reshape(M * SH, DH)
        out[...] = (pairs.T * factor).astype(BF16)

    send_last(1, dv_acc[...])

    for batch in (0, 1):
        for j in range(1, M):
            stats_copy(batch, j, False).wait_recv()
    stats_in[share] = stats[...]

    def one_shift(m, carry):
        total = jnp.zeros((8, DH), F32)
        for src in range(M):
            back = place((src // 2 + 4 - m // 2) % 4)
            total = total + stats_in[src, back * 2 + (src + m) % 2]
        shift = total[0:4] / jnp.maximum(total[4:8], 1.0)
        shifts[m] = wide(shift, 0)
        return carry

    lax.fori_loop(0, M, one_shift, 0)

    def second_pass(m):
        row_shift = shifts[m]
        for j in range(KN // 8):
            lo = j * 8
            probs[lo : lo + 8, :] = w_all[m, lo : lo + 8, :] * (dp_all[m, lo : lo + 8, :] - row_shift)
        ds = probs[...].astype(BF16)
        dk_acc[...] += dot(ds, gq[m])
        return dot(kt[...], ds)

    def core_copy(yy):
        return send(dq_mate_out.at[yy], dq_mate_in.at[yy], c_send.at[yy], c_recv.at[yy], mate, c)

    def dq_copy(t, out):
        step = (1, 3, 2)[t - 1]
        to_y = (y + 4 - step) % 4
        if out:
            return send(dq_sum.at[to_y], dq_in.at[t - 1], d_send.at[t - 1], d_recv.at[t - 1], row_of(to_y, core), c)
        frm_y = (y + step) % 4
        return send(dq_sum.at[y], dq_in.at[t - 1], d_send.at[t - 1], d_recv.at[t - 1], row_of(frm_y, core), c)

    def add_mate(t):
        yy = (y + 4 - (0, 1, 3, 2)[t]) % 4
        core_copy(yy).wait_recv()
        dq_sum[yy] = (dq_mine[yy] + dq_mate_in[yy].astype(F32)).astype(BF16)
        if t:
            dq_copy(t, True).start()

    def pass_two(i, carry):
        yy = (y + 4 - place(3 - i // 2)) % 4
        part = second_pass(yy * 2 + (other + i) % 2)

        @pl.when(i % 2 == 0)
        def _():
            dq_mate_out[yy] = part.astype(BF16)
            core_copy(yy).start()

        @pl.when(i % 2 == 1)
        def _():
            dq_mine[yy] = part

        @pl.when(i == 3)
        def _():
            add_mate(3)

        @pl.when(i == 5)
        def _():
            add_mate(2)

        return carry

    lax.fori_loop(0, M, pass_two, 0)
    send_last(0, dk_acc[...])
    add_mate(1)
    add_mate(0)
    finish(1, dv_out, 1.0)
    dq = dq_sum[y].astype(F32)
    for t in (3, 2, 1):
        dq_copy(t, False).wait_recv()
        dq = dq + dq_in[t - 1].astype(F32)
    dq_out[...] = (dq * FACTOR).astype(BF16)
    finish(0, dk_out, FACTOR)

    for kind, buf in both:
        for t in (1, 2, 3):
            y_copy(kind, buf, t, True).wait_send()
        for t in range(4):
            mate_copy(kind, buf, t, True).wait_send()
    for kind in (0, 1, 2):
        for j in far_first:
            col_copy(kind, j, True).wait_send()
    for j in range(1, M):
        info_copy(j, True).wait_send()
        stats_copy(0, j, True).wait_send()
        stats_copy(1, j, True).wait_send()
    for yy in range(4):
        core_copy(yy).wait_send()
    for t in (1, 2, 3):
        dq_copy(t, True).wait_send()
    for kind in (0, 1):
        for j in range(1, N):
            last_copy(kind, j, True).wait_send()

    @pl.when(c != r)
    def _():
        for kind in (0, 1):
            last_copy(kind, 0, True).wait_send()


def local(*args):
    hbm = pl.BlockSpec(memory_space=pltpu.HBM)
    vmem = pl.BlockSpec(memory_space=pltpu.VMEM)
    V = pltpu.VMEM
    S = pltpu.SMEM
    dma = pltpu.SemaphoreType.DMA
    return pl.pallas_call(
        kernel,
        out_shape=(
            jax.ShapeDtypeStruct((DH, QN), BF16),
            jax.ShapeDtypeStruct((DH, 2 * BLK), BF16),
            jax.ShapeDtypeStruct((DH, 2 * BLK), BF16),
        ),
        in_specs=[hbm] * 8,
        out_specs=(vmem,) * 3,
        scratch_shapes=[
            S((N,), F32), S((4,), jnp.int32), S((2,), jnp.int32), V((N, QN), F32),
            V((N, SH, DH), BF16), V((N, SH, DH), BF16), V((N, 8, DH), F32), V((8, DH), F32),
            V((M, QN, DH), BF16), V((M, QN, DH), BF16), V((M, 8, DH), F32),
            V((DH, KN), BF16), V((M, KN, QN), F32), V((M, KN, QN), F32), V((KN, QN), F32),
            V((KN, DH), F32), V((KN, DH), F32), V((M, 8, DH), F32), V((M, M, 8, DH), F32), V((M, 8, QN), F32),
            V((4, DH, QN), F32), V((4, DH, QN), BF16), V((4, DH, QN), BF16), V((4, DH, QN), BF16), V((3, DH, QN), BF16),
            V((N, SH, DH), BF16), V((N, SH, DH), BF16), V((N, SH, DH), BF16), V((N, SH, DH), BF16),
            dma((8,)), dma((3, N)), dma((3, N)), dma((2, 3)), dma((2, 3)), dma((2, 4)), dma((2, 4)),
            dma((M,)), dma((M,)), dma((2, M)), dma((2, M)),
            dma((4,)), dma((4,)), dma((3,)), dma((3,)), dma((2, N)), dma((2, N)),
        ],
        compiler_params=pltpu.CompilerParams(
            collective_id=0, has_side_effects=True, vmem_limit_bytes=48 * 1024 * 1024
        ),
    )(*[pltpu.with_memory_space_constraint(a, pltpu.HBM) for a in args])


def solution(mesh):
    in_specs = (
        P("row", None), P("col", None), P("col", None), P("row", None),
        P(None, "row"), P(), P("row"), P("col"),
    )
    out_specs = (P("col", "row"), P("row", "col"), P("row", "col"))
    return jax.shard_map(local, mesh=mesh, in_specs=in_specs, out_specs=out_specs, check_vma=False)
```

```python
import math

import jax
import jax.numpy as jnp
from jax import lax
from jax.experimental import pallas as pl
from jax.experimental.pallas import tpu as pltpu
from jax.sharding import PartitionSpec as P

MESH = pl.DeviceIdType.MESH
DH = 128
BLK = 128
QN = 512
N = 16
SH = 32
KN = N * SH
M = 8
F32 = jnp.float32
BF16 = jnp.bfloat16
FACTOR = 1.0 / math.sqrt(DH)


def dot(a, b):
    return jnp.dot(a, b, preferred_element_type=F32)


def dot_nt(a, b):
    return lax.dot_general(a, b, (((1,), (1,)), ((), ())), preferred_element_type=F32)


def place(t):
    return t + t // 2 - 2 * (t // 3)


def kernel(
    queries, keys, values, out_grad, tau_in, alpha_in, query_blocks_in, key_blocks_in,
    dq_out, dk_out, dv_out,
    alpha, query_blocks, key_blocks, tau,
    gk, gv, gb, gb_send,
    gq, gg, info,
    kt, w_all, dp_all, probs, dv_acc, dk_acc, stats, stats_in, shifts,
    dq_mine, dq_mate_out, dq_mate_in, dq_sum, dq_in, own_k, own_v, row_k, row_v,
    in_sem, a_send, a_recv, y_send, y_recv, m_send, m_recv, i_send, i_recv, s_send, s_recv,
    c_send, c_recv, d_send, d_recv, p_send, p_recv,
):
    r = lax.axis_index("row")
    c = lax.axis_index("col")
    y = r // 4
    xh = (r // 2) % 2
    core = r % 2
    other = 1 - core
    share = y * 2 + core

    def row_of(yy, cc):
        return yy * 4 + xh * 2 + cc

    mate = row_of(y, other)

    def send(src, dst, ssem, rsem, row, col):
        return pltpu.make_async_remote_copy(
            src_ref=src, dst_ref=dst, send_sem=ssem, recv_sem=rsem,
            device_id=(row, col), device_id_type=MESH,
        )

    def member(j):
        yy = (y + j // 2) % 4
        cc = (core + j) % 2
        return yy, cc, yy * 2 + cc

    barrier = pltpu.get_barrier_semaphore()

    def greet(row, col):
        pl.semaphore_signal(barrier, inc=1, device_id=(row, col), device_id_type=MESH)

    for j in range(1, N):
        greet(r, (c + j) % N)
    for j in range(1, M):
        yy, cc, _ = member(j)
        greet(row_of(yy, cc), c)
    for j in range(1, N):
        greet((r + j) % N, r)

    @pl.when(c != r)
    def _():
        greet(r, r)

    key_rows = pl.ds(pl.multiple_of(share * SH, SH), SH)

    def head(h):
        return pl.ds(pl.multiple_of(h * DH, DH), DH)

    loads = [
        pltpu.make_async_copy(key_blocks_in, key_blocks, in_sem.at[0]),
        pltpu.make_async_copy(query_blocks_in, query_blocks, in_sem.at[1]),
        pltpu.make_async_copy(alpha_in, alpha, in_sem.at[2]),
        pltpu.make_async_copy(tau_in, tau, in_sem.at[3]),
        pltpu.make_async_copy(queries.at[:, head(c)], gq.at[share], in_sem.at[4]),
        pltpu.make_async_copy(out_grad.at[:, head(c)], gg.at[share], in_sem.at[5]),
        pltpu.make_async_copy(keys.at[key_rows, head(c)], gk.at[c], in_sem.at[6]),
        pltpu.make_async_copy(values.at[key_rows, head(c)], gv.at[c], in_sem.at[7]),
    ]
    for load in loads:
        load.start()
    apart = ((c + N - r) % N + N - 1) // N
    pl.semaphore_wait(barrier, (N - 1) + (M - 1) + (N - 1) + apart)

    def col_copy(kind, j, out):
        peer = (c + j) % N
        frm = c if out else peer
        src, dst = (
            (keys.at[key_rows, head(peer)], gk.at[frm]),
            (values.at[key_rows, head(peer)], gv.at[frm]),
            (gb_send, gb.at[frm]),
        )[kind]
        return send(src, dst, a_send.at[kind, j], a_recv.at[kind, frm], r, peer)

    far_first = sorted(range(1, N), key=lambda j: -min(j, N - j))

    both = ((0, gq), (1, gg))
    own = (queries, out_grad)
    HALF = (pl.ds(0, QN // 2), pl.ds(QN // 2, QN // 2))

    def y_copy(kind, way, stage, out):
        buf = both[kind][1]
        step = 1 if way == 0 else 3
        part = HALF[way] if stage != 1 else HALF[1 - way]
        sem = (kind, way, stage)
        back = (1 if stage < 2 else 2) * (4 - step)
        if out and stage == 2:
            m = ((y + 4 - step) % 4) * 2 + core
        else:
            m = share if out else ((y + back) % 4) * 2 + core
        dst = buf.at[m, part]
        src = own[kind].at[part, head(c)] if out and stage < 2 else dst
        peer = (y + step) % 4 if out else (y + 4 - step) % 4
        return send(src, dst, y_send.at[sem], y_recv.at[sem], row_of(peer, core), c)

    def mate_copy(kind, t, part, out):
        buf = both[kind][1]
        yy = (y + 4 - (0, 1, 3, 2)[t]) % 4
        dst = buf.at[yy * 2 + (core if out else other), HALF[part]]
        src = own[kind].at[HALF[part], head(c)] if out and t == 0 else dst
        return send(src, dst, m_send.at[kind, t, part], m_recv.at[kind, t, part], mate, c)

    def info_copy(j, out):
        yy, cc, m = member(j)
        frm = share if out else m
        return send(info.at[frm], info.at[frm], i_send.at[m], i_recv.at[frm], row_of(yy, cc), c)

    for j in far_first:
        col_copy(0, j, True).start()
    for kind in (0, 1):
        for way in (0, 1):
            y_copy(kind, way, 0, True).start()
    for load in loads[:4]:
        load.wait()
    base = (key_blocks[share // 4] * BLK + (share % 4) * SH).astype(F32)
    gb_send[...] = jnp.full((1, DH), base)
    gb[c] = gb_send[...]
    line = tau[pl.ds(c, 1), :]
    for i in range(4):
        info[share, i : i + 1, :] = line[:, i * DH : (i + 1) * DH]
        info[share, 4 + i : 5 + i, :] = jnp.full((1, DH), query_blocks[i] * BLK).astype(F32)
    for j in far_first:
        col_copy(2, j, True).start()
    for j in range(1, M):
        info_copy(j, True).start()
    for j in far_first:
        col_copy(1, j, True).start()
    for kind in (0, 1):
        for way in (0, 1):
            y_copy(kind, way, 1, True).start()
    for kind in (0, 1):
        for part in (0, 1):
            mate_copy(kind, 0, part, True).start()

    dv_acc[...] = jnp.zeros_like(dv_acc)
    dk_acc[...] = jnp.zeros_like(dk_acc)
    excess = jnp.full((8, QN), alpha[c]) - 1.0
    scale = excess * FACTOR
    power = (1.0 - excess) / excess * (1.0 / math.log(2.0))
    lane = lax.broadcasted_iota(jnp.int32, (8, QN), 1) % BLK
    row8 = lax.broadcasted_iota(jnp.int32, (8, QN), 0)
    ahead = (lane - row8).astype(F32)

    def wide(tile, lo):
        line = jnp.concatenate([tile[lo + i : lo + i + 1, :] for i in range(4)], axis=1)
        return jnp.broadcast_to(line, (8, QN))

    def arrived(way, stage):
        t = (3 if stage == 2 else 1 + way)
        part = way if stage != 1 else 1 - way
        for kind in (0, 1):
            y_copy(kind, way, stage, False).wait_recv()
            if stage == 0:
                y_copy(kind, way, 2, True).start()
            mate_copy(kind, t, part, True).start()

    def from_mate(t):
        for kind in (0, 1):
            for part in (0, 1):
                mate_copy(kind, t, part, False).wait_recv()

    for load in loads[4:]:
        load.wait()
    for way in (0, 1):
        arrived(way, 0)
    for j in range(1, M):
        info_copy(j, False).wait_recv()
    for kind in (0, 2):
        for j in far_first:
            col_copy(kind, j, False).wait_recv()
    kt[...] = gk[...].reshape(KN, DH).T

    def lines(total):
        total = jnp.sum(total, axis=0, keepdims=True)
        return jnp.concatenate([total[:, i * DH : (i + 1) * DH] for i in range(4)], axis=0)

    def weigh(m, spot):
        scores = dot_nt(gk[...].reshape(KN, DH), gq[m])
        tile = info[m]
        shift_in = wide(tile, 0) * excess
        query = wide(tile, 4) + ahead
        m_sum = jnp.zeros((8, QN), F32)
        for j in range(N):
            b = jnp.broadcast_to(jnp.concatenate([gb[j]] * (QN // DH), axis=1), (8, QN))
            for i in range(SH // 16):
                pair = []
                for lo in (j * SH + i * 16, j * SH + i * 16 + 8):
                    x = scores[lo : lo + 8] * scale - shift_in
                    x = jnp.where(b + (lo - j * SH) <= query, jnp.maximum(x, 0.0), 0.0)
                    w = jnp.exp2(jnp.log(x) * power)
                    w_all[m, lo : lo + 8, :] = w
                    pair.append(w * x)
                    m_sum = m_sum + w
                probs[lo - 8 : lo + 8, :] = jnp.concatenate(pair, axis=0).astype(BF16)
        dv_acc[...] += dot(probs[...], gg[m])
        stats[spot, 4:8, :] = lines(m_sum)

    def match(m, spot):
        dp = dot_nt(gv[...].reshape(KN, DH), gg[m])
        dp_all[m] = dp
        t_sum = jnp.zeros((8, QN), F32)
        for lo in range(0, KN, 8):
            t_sum = t_sum + w_all[m, lo : lo + 8, :] * dp[lo : lo + 8]
        stats[spot, 0:4, :] = lines(t_sum)

    BATCH = ((0, 6), (6, 8))

    def stats_copy(batch, j, out):
        yy, cc, m = member(j)
        frm = share if out else m
        lo, hi = BATCH[batch]
        return send(
            stats.at[lo:hi], stats_in.at[frm, lo:hi], s_send.at[batch, m], s_recv.at[batch, frm], row_of(yy, cc), c
        )

    def spot_of(t, half):
        yy = (y + 4 - place(t)) % 4
        return yy * 2 + (core + half) % 2, 2 * t + half

    def early(i):
        return spot_of(i // 2 + i // 3, (i % 2) * (1 - i // 2))

    def late(i):
        return spot_of(i + 1 - i // 3, 1 - (i // 2) * (1 - i % 2))

    def weigh_early(i, carry):
        @pl.when(i == 1)
        def _():
            from_mate(0)

        for way in (0, 1):

            @pl.when(i == 2 + way)
            def _():
                arrived(way, 1)

        weigh(*early(i))
        return carry

    lax.fori_loop(0, 4, weigh_early, 0)
    for j in far_first:
        col_copy(1, j, False).wait_recv()

    def match_early(i, carry):
        match(*early(i))
        return carry

    lax.fori_loop(0, 4, match_early, 0)
    for way in (0, 1):
        arrived(way, 2)

    def both_late(i, carry):
        for step, t in ((0, 1), (1, 2), (3, 3)):

            @pl.when(i == step)
            def _():
                from_mate(t)

        m, spot = late(i)
        weigh(m, spot)
        match(m, spot)

        @pl.when(i == 1)
        def _():
            for j in range(1, M):
                stats_copy(0, j, True).start()

        return carry

    lax.fori_loop(0, 4, both_late, 0)
    for j in range(1, M):
        stats_copy(1, j, True).start()

    def last_copy(kind, j, out):
        src, dst = ((own_k, row_k), (own_v, row_v))[kind]
        if out:
            peer = (c + j) % N
            return send(src.at[peer], dst.at[r], p_send.at[kind, j], p_recv.at[kind, r], c, peer)
        peer = (r + j) % N
        return send(src.at[c], dst.at[peer], p_send.at[kind, j], p_recv.at[kind, peer], peer, r)

    def send_last(kind, total):
        src, dst = ((own_k, row_k), (own_v, row_v))[kind]
        src[...] = total.astype(BF16).reshape(N, SH, DH)
        for j in range(1, N):
            last_copy(kind, j, True).start()

        @pl.when(c != r)
        def _():
            last_copy(kind, 0, True).start()

        @pl.when(c == r)
        def _():
            dst[r] = src[c]

    def finish(kind, out, factor):
        for j in range(1, N):
            last_copy(kind, j, False).wait_recv()

        @pl.when(c != r)
        def _():
            last_copy(kind, 0, False).wait_recv()

        final = (row_k, row_v)[kind]
        pairs = final[...].astype(F32).reshape(4, 2, 2, SH, DH)
        pairs = (pairs[:, 0] + pairs[:, 1]).reshape(M * SH, DH)
        out[...] = (pairs.T * factor).astype(BF16)

    send_last(1, dv_acc[...])

    for batch in (0, 1):
        for j in range(1, M):
            stats_copy(batch, j, False).wait_recv()
    stats_in[share] = stats[...]

    def one_shift(m, carry):
        total = jnp.zeros((8, DH), F32)
        for src in range(M):
            back = place((src // 2 + 4 - m // 2) % 4)
            total = total + stats_in[src, back * 2 + (src + m) % 2]
        shift = total[0:4] / jnp.maximum(total[4:8], 1.0)
        shifts[m] = wide(shift, 0)
        return carry

    lax.fori_loop(0, M, one_shift, 0)

    def second_pass(m):
        row_shift = shifts[m]
        for lo in range(0, KN, 16):
            pair = [w_all[m, i : i + 8, :] * (dp_all[m, i : i + 8, :] - row_shift) for i in (lo, lo + 8)]
            probs[lo : lo + 16, :] = jnp.concatenate(pair, axis=0).astype(BF16)
        ds = probs[...]
        dk_acc[...] += dot(ds, gq[m])
        return dot(kt[...], ds)

    def core_copy(yy):
        return send(dq_mate_out.at[yy], dq_mate_in.at[yy], c_send.at[yy], c_recv.at[yy], mate, c)

    def dq_copy(t, out):
        step = (1, 3, 2)[t - 1]
        to_y = (y + 4 - step) % 4
        if out:
            return send(dq_sum.at[to_y], dq_in.at[t - 1], d_send.at[t - 1], d_recv.at[t - 1], row_of(to_y, core), c)
        frm_y = (y + step) % 4
        return send(dq_sum.at[y], dq_in.at[t - 1], d_send.at[t - 1], d_recv.at[t - 1], row_of(frm_y, core), c)

    def add_mate(t):
        yy = (y + 4 - (0, 1, 3, 2)[t]) % 4
        core_copy(yy).wait_recv()
        dq_sum[yy] = (dq_mine[yy] + dq_mate_in[yy].astype(F32)).astype(BF16)
        if t:
            dq_copy(t, True).start()

    def pass_two(i, carry):
        yy = (y + 4 - place(3 - i // 2)) % 4
        part = second_pass(yy * 2 + (other + i) % 2)

        @pl.when(i % 2 == 0)
        def _():
            dq_mate_out[yy] = part.astype(BF16)
            core_copy(yy).start()

        @pl.when(i % 2 == 1)
        def _():
            dq_mine[yy] = part

        @pl.when(i == 3)
        def _():
            add_mate(3)

        @pl.when(i == 5)
        def _():
            add_mate(2)

        return carry

    lax.fori_loop(0, M, pass_two, 0)
    send_last(0, dk_acc[...])
    add_mate(1)
    add_mate(0)
    finish(1, dv_out, 1.0)
    dq = dq_sum[y].astype(F32)
    for t in (3, 2, 1):
        dq_copy(t, False).wait_recv()
        dq = dq + dq_in[t - 1].astype(F32)
    dq_out[...] = (dq * FACTOR).astype(BF16)
    finish(0, dk_out, FACTOR)

    for kind in (0, 1):
        for way in (0, 1):
            for stage in (0, 1, 2):
                y_copy(kind, way, stage, True).wait_send()
        for t in range(4):
            for part in (0, 1):
                mate_copy(kind, t, part, True).wait_send()
    for kind in (0, 1, 2):
        for j in far_first:
            col_copy(kind, j, True).wait_send()
    for j in range(1, M):
        info_copy(j, True).wait_send()
        stats_copy(0, j, True).wait_send()
        stats_copy(1, j, True).wait_send()
    for yy in range(4):
        core_copy(yy).wait_send()
    for t in (1, 2, 3):
        dq_copy(t, True).wait_send()
    for kind in (0, 1):
        for j in range(1, N):
            last_copy(kind, j, True).wait_send()

    @pl.when(c != r)
    def _():
        for kind in (0, 1):
            last_copy(kind, 0, True).wait_send()


def local(*args):
    hbm = pl.BlockSpec(memory_space=pltpu.HBM)
    vmem = pl.BlockSpec(memory_space=pltpu.VMEM)
    V = pltpu.VMEM
    S = pltpu.SMEM
    dma = pltpu.SemaphoreType.DMA
    return pl.pallas_call(
        kernel,
        out_shape=(
            jax.ShapeDtypeStruct((DH, QN), BF16),
            jax.ShapeDtypeStruct((DH, 2 * BLK), BF16),
            jax.ShapeDtypeStruct((DH, 2 * BLK), BF16),
        ),
        in_specs=[hbm] * 8,
        out_specs=(vmem,) * 3,
        scratch_shapes=[
            S((N,), F32), S((4,), jnp.int32), S((2,), jnp.int32), V((N, QN), F32),
            V((N, SH, DH), BF16), V((N, SH, DH), BF16), V((N, 1, DH), F32), V((1, DH), F32),
            V((M, QN, DH), BF16), V((M, QN, DH), BF16), V((M, 8, DH), F32),
            V((DH, KN), BF16), V((M, KN, QN), F32), V((M, KN, QN), F32), V((KN, QN), BF16),
            V((KN, DH), F32), V((KN, DH), F32), V((M, 8, DH), F32), V((M, M, 8, DH), F32), V((M, 8, QN), F32),
            V((4, DH, QN), F32), V((4, DH, QN), BF16), V((4, DH, QN), BF16), V((4, DH, QN), BF16), V((3, DH, QN), BF16),
            V((N, SH, DH), BF16), V((N, SH, DH), BF16), V((N, SH, DH), BF16), V((N, SH, DH), BF16),
            dma((8,)), dma((3, N)), dma((3, N)), dma((2, 2, 3)), dma((2, 2, 3)), dma((2, 4, 2)), dma((2, 4, 2)),
            dma((M,)), dma((M,)), dma((2, M)), dma((2, M)),
            dma((4,)), dma((4,)), dma((3,)), dma((3,)), dma((2, N)), dma((2, N)),
        ],
        compiler_params=pltpu.CompilerParams(
            collective_id=0, has_side_effects=True, vmem_limit_bytes=48 * 1024 * 1024
        ),
    )(*[pltpu.with_memory_space_constraint(a, pltpu.HBM) for a in args])


def solution(mesh):
    in_specs = (
        P("row", None), P("col", None), P("col", None), P("row", None),
        P(None, "row"), P(), P("row"), P("col"),
    )
    out_specs = (P("col", "row"), P("row", "col"), P("row", "col"))
    return jax.shard_map(local, mesh=mesh, in_specs=in_specs, out_specs=out_specs, check_vma=False)
```

```python
import math

import jax
import jax.numpy as jnp
from jax import lax
from jax.experimental import pallas as pl
from jax.experimental.pallas import tpu as pltpu
from jax.sharding import PartitionSpec as P

MESH = pl.DeviceIdType.MESH
DH = 128
BLK = 128
QN = 512
N = 16
SH = 32
KN = N * SH
Y = 4
F32 = jnp.float32
BF16 = jnp.bfloat16
FACTOR = 1.0 / math.sqrt(DH)


def dot(a, b):
    return jnp.dot(a, b, preferred_element_type=F32)


def dot_nt(a, b):
    return lax.dot_general(a, b, (((1,), (1,)), ((), ())), preferred_element_type=F32)


def place(t):
    return t + t // 2 - 2 * (t // 3)


def kernel(
    queries, keys, values, out_grad, tau_in, alpha_in, query_blocks_in, key_blocks_in,
    dq_out, dk_out, dv_out,
    alpha, query_blocks, key_blocks, tau,
    gk, gv, gb, gb_send,
    gq, gg, info,
    kt, w_all, dp_all, probs, dscore, dv_acc, dk_acc, dq_acc, stats, stats_in, shifts,
    core_out, core_in, dq_send, dq_in, own_part, row_part,
    in_sem, a_send, a_recv, x_send, x_recv, y_send, y_recv, i_send, i_recv, s_send, s_recv,
    c_send, c_recv, d_send, d_recv, p_send, p_recv,
):
    r = lax.axis_index("row")
    c = lax.axis_index("col")
    y = r // 4
    xh = (r // 2) % 2
    core = r % 2
    other = 1 - core
    share = y * 2 + core

    def row_of(yy, cc):
        return yy * 4 + xh * 2 + cc

    mate = row_of(y, other)

    def send(src, dst, ssem, rsem, row, col):
        return pltpu.make_async_remote_copy(
            src_ref=src, dst_ref=dst, send_sem=ssem, recv_sem=rsem,
            device_id=(row, col), device_id_type=MESH,
        )

    def landed(sem, ref):
        send(ref, ref, in_sem.at[0], sem, mate, c).wait_recv()

    def left(sem, ref):
        send(ref, ref, sem, in_sem.at[0], mate, c).wait_send()

    barrier = pltpu.get_barrier_semaphore()

    def greet(row, col):
        pl.semaphore_signal(barrier, inc=1, device_id=(row, col), device_id_type=MESH)

    for j in range(1, N):
        greet(r, (c + j) % N)
    for j in range(1, Y):
        greet(row_of((y + j) % Y, core), c)
    greet(mate, c)
    for j in range(1, N):
        greet((r + j) % N, r)

    @pl.when(c != r)
    def _():
        greet(r, r)

    key_rows = pl.ds(pl.multiple_of(share * SH, SH), SH)

    def head(h):
        return pl.ds(pl.multiple_of(h * DH, DH), DH)

    loads = [
        pltpu.make_async_copy(key_blocks_in, key_blocks, in_sem.at[0]),
        pltpu.make_async_copy(query_blocks_in, query_blocks, in_sem.at[1]),
        pltpu.make_async_copy(alpha_in, alpha, in_sem.at[2]),
        pltpu.make_async_copy(tau_in, tau, in_sem.at[3]),
        pltpu.make_async_copy(queries.at[:, head(c)], gq.at[y], in_sem.at[4]),
        pltpu.make_async_copy(out_grad.at[:, head(c)], gg.at[y], in_sem.at[5]),
        pltpu.make_async_copy(keys.at[key_rows, head(c)], gk.at[0, c], in_sem.at[6]),
        pltpu.make_async_copy(values.at[key_rows, head(c)], gv.at[0, c], in_sem.at[7]),
    ]
    for load in loads:
        load.start()
    apart = ((c + N - r) % N + N - 1) // N
    pl.semaphore_wait(barrier, (N - 1) + Y + (N - 1) + apart)

    far_first = sorted(range(1, N), key=lambda j: -min(j, N - j))

    def to_columns(kind):
        for j in far_first:
            peer = (c + j) % N
            src, dst = (
                (keys.at[key_rows, head(peer)], gk.at[0, c]),
                (values.at[key_rows, head(peer)], gv.at[0, c]),
                (gb_send, gb.at[c]),
            )[kind]
            send(src, dst, a_send.at[kind], a_recv.at[kind], r, peer).start()

    own = (queries, out_grad)
    group = (gq, gg)
    HALF = (pl.ds(0, QN // 2), pl.ds(QN // 2, QN // 2))

    def along_y(way, stage):
        step = 1 if way == 0 else 3
        part = HALF[way] if stage != 1 else HALF[1 - way]
        m = y if stage < 2 else (y + 4 - step) % Y
        for kind in (0, 1):
            dst = group[kind].at[m, part]
            src = own[kind].at[part, head(c)] if stage < 2 else dst
            send(
                src, dst, y_send.at[stage // 2], y_recv.at[way, stage], row_of((y + step) % Y, core), c
            ).start()

    def from_y(way, stage):
        landed(y_recv.at[way, stage], gq.at[0])

    to_columns(0)
    for way in (0, 1):
        along_y(way, 0)
    for load in loads[:4]:
        load.wait()
    base = (key_blocks[share // 4] * BLK + (share % 4) * SH).astype(F32)
    gb_send[...] = jnp.full((1, DH), base)
    gb[c] = gb_send[...]
    line = tau[pl.ds(c, 1), :]
    for i in range(4):
        info[y, i : i + 1, :] = line[:, i * DH : (i + 1) * DH]
        info[y, 4 + i : 5 + i, :] = jnp.full((1, DH), query_blocks[i] * BLK).astype(F32)
    to_columns(2)
    for j in range(1, Y):
        send(info.at[y], info.at[y], i_send, i_recv, row_of((y + j) % Y, core), c).start()
    to_columns(1)
    for way in (0, 1):
        along_y(way, 1)

    dk_acc[...] = jnp.zeros_like(dk_acc)
    excess = jnp.full((8, QN), alpha[c]) - 1.0
    scale = excess * FACTOR
    power = (1.0 - excess) / excess * (1.0 / math.log(2.0))
    lane = lax.broadcasted_iota(jnp.int32, (8, QN), 1) % BLK
    row8 = lax.broadcasted_iota(jnp.int32, (8, QN), 0)
    ahead = (lane - row8).astype(F32)

    def wide(tile, lo):
        line = jnp.concatenate([tile[lo + i : lo + i + 1, :] for i in range(4)], axis=1)
        return jnp.broadcast_to(line, (8, QN))

    for load in loads[4:]:
        load.wait()
    for way in (0, 1):
        from_y(way, 0)
        along_y(way, 2)
    landed(i_recv, info.at[0:3])
    landed(a_recv.at[0], gk.at[0, 0 : N - 1])
    to_mate_k = send(gk.at[0], gk.at[1], x_send.at[0], x_recv.at[0], mate, c)
    to_mate_v = send(gv.at[0], gv.at[1], x_send.at[1], x_recv.at[1], mate, c)
    to_mate_k.start()
    kt[0] = gk[0].reshape(KN, DH).T
    landed(a_recv.at[2], gb.at[0 : N - 1])

    def lines(total):
        total = jnp.sum(total, axis=0, keepdims=True)
        return jnp.concatenate([total[:, i * DH : (i + 1) * DH] for i in range(4)], axis=0)

    def member(t):
        return (y + 4 - place(t)) % Y

    def weigh(h, t):
        m = member(t)
        scores = dot_nt(gk[h].reshape(KN, DH), gq[m])
        tile = info[m]
        shift_in = wide(tile, 0) * excess
        query = wide(tile, 4) + ahead - (h * SH * (other - core)).astype(F32)
        m_sum = jnp.zeros((8, QN), F32)
        for j in range(N):
            b = jnp.broadcast_to(jnp.concatenate([gb[j]] * (QN // DH), axis=1), (8, QN))
            for i in range(SH // 16):
                pair = []
                for lo in (j * SH + i * 16, j * SH + i * 16 + 8):
                    x = scores[lo : lo + 8] * scale - shift_in
                    x = jnp.where(b + (lo - j * SH) <= query, jnp.maximum(x, 0.0), 0.0)
                    w = jnp.exp2(jnp.log(x) * power)
                    w_all[h, t, lo : lo + 8, :] = w
                    pair.append(w * x)
                    m_sum = m_sum + w
                probs[h, t, lo - 8 : lo + 8, :] = jnp.concatenate(pair, axis=0).astype(BF16)
        stats[h, t, 4:8, :] = lines(m_sum)

    def match(h, t):
        dp = dot_nt(gv[h].reshape(KN, DH), gg[member(t)])
        dp_all[h, t] = dp
        t_sum = jnp.zeros((8, QN), F32)
        for lo in range(0, KN, 8):
            t_sum = t_sum + w_all[h, t, lo : lo + 8, :] * dp[lo : lo + 8]
        stats[h, t, 0:4, :] = lines(t_sum)

    def sums_to_y(lo, hi):
        stats[0, lo:hi] = stats[0, lo:hi] + stats[1, lo:hi]
        for j in range(1, Y):
            send(
                stats.at[0, lo:hi], stats_in.at[y, lo:hi], s_send.at[lo // 3], s_recv.at[lo // 3],
                row_of((y + j) % Y, core), c,
            ).start()

    def weigh_early(i, carry):
        for way in (0, 1):

            @pl.when(i == 1 + way)
            def _():
                from_y(way, 1)

        @pl.when(i == 3)
        def _():
            landed(x_recv.at[0], gk.at[1])

        @pl.when(i == 4)
        def _():
            landed(a_recv.at[1], gv.at[0, 0 : N - 1])
            to_mate_v.start()

        weigh(i // 3, i % 3)
        return carry

    def match_early(i, carry):
        match(0, i)
        return carry

    def weigh_late(i, carry):
        weigh(i, 3)
        return carry

    def match_late(i, carry):
        @pl.when(i == 1)
        def _():
            landed(x_recv.at[1], gv.at[1])

        h = 1 - (4 - i) // 4
        match(h, 3 * (1 - h) + (i - 1) * h)

        @pl.when(i == 3)
        def _():
            sums_to_y(0, 3)

        return carry

    lax.fori_loop(0, 6, weigh_early, 0)
    lax.fori_loop(0, 3, match_early, 0)
    for way in (0, 1):
        from_y(way, 2)
    lax.fori_loop(0, 2, weigh_late, 0)
    lax.fori_loop(0, 5, match_late, 0)
    sums_to_y(3, 4)
    kt[1] = gk[1].reshape(KN, DH).T

    def core_copy(kind):
        return send(core_out.at[kind], core_in.at[kind], c_send.at[kind], c_recv.at[kind], mate, c)

    def add_values(i, carry):
        h = 1 - i // Y
        t = i % Y

        @pl.when(t == 0)
        def _():
            dv_acc[...] = jnp.zeros_like(dv_acc)

        dv_acc[...] += dot(probs[h, t], gg[member(t)])

        @pl.when(i == Y - 1)
        def _():
            core_out[1] = dv_acc[...].astype(BF16)
            core_copy(1).start()

        return carry

    lax.fori_loop(0, 2 * Y, add_values, 0)

    def send_last(kind, total):
        landed(c_recv.at[kind], core_in.at[kind])
        total = total + core_in[kind].astype(F32)
        own_part[kind] = total.astype(BF16).reshape(N, SH, DH)

        def one(j):
            peer = (c + j) % N
            send(
                own_part.at[kind, peer], row_part.at[kind, r], p_send.at[kind], p_recv.at[kind], c, peer
            ).start()

        for j in range(1, N):
            one(j)

        @pl.when(c != r)
        def _():
            one(0)

        @pl.when(c == r)
        def _():
            row_part[kind, r] = own_part[kind, c]

    def finish(kind, out, factor):
        @pl.when(c != r)
        def _():
            landed(p_recv.at[kind], row_part.at[kind])

        @pl.when(c == r)
        def _():
            landed(p_recv.at[kind], row_part.at[kind, 0 : N - 1])

        pairs = row_part[kind].astype(F32).reshape(4, 2, 2, SH, DH)
        pairs = (pairs[:, 0] + pairs[:, 1]).reshape(8 * SH, DH)
        out[...] = (pairs.T * factor).astype(BF16)

    landed(s_recv.at[0], stats_in.at[0:3, 0:3])
    landed(s_recv.at[1], stats_in.at[0:3, 3:4])
    stats_in[y] = stats[0]

    def one_shift(t, carry):
        m = member(t)
        total = jnp.zeros((8, DH), F32)
        for src in range(Y):
            total = total + stats_in[src, place((src + 4 - m) % Y)]
        shift = total[0:4] / jnp.maximum(total[4:8], 1.0)
        shifts[t] = wide(shift, 0)
        return carry

    lax.fori_loop(0, Y, one_shift, 0)

    def second_pass(h, t):
        row_shift = shifts[t]
        for lo in range(0, KN, 16):
            pair = [w_all[h, t, i : i + 8, :] * (dp_all[h, t, i : i + 8, :] - row_shift) for i in (lo, lo + 8)]
            dscore[lo : lo + 16, :] = jnp.concatenate(pair, axis=0).astype(BF16)
        ds = dscore[...]
        dk_acc[h] += dot(ds, gq[member(t)])
        return dot(kt[h], ds)

    def pass_two(i, carry):
        h = 1 - i // Y
        t = 3 - i % Y
        part = second_pass(h, t)

        @pl.when(h == 1)
        def _():
            dq_acc[t] = part

        @pl.when(i == Y - 1)
        def _():
            core_out[0] = dk_acc[1].astype(BF16)
            core_copy(0).start()

        @pl.when(h == 0)
        def _():
            dq_acc[t] += part
            dq_send[t] = dq_acc[t].astype(BF16)

        for tt in (3, 2, 1):

            @pl.when(i == 2 * Y - 1 - tt)
            def _():
                send(dq_send.at[tt], dq_in.at[tt - 1], d_send, d_recv, row_of(member(tt), core), c).start()

        @pl.when(i == 1)
        def _():
            send_last(1, dv_acc[...])

        return carry

    lax.fori_loop(0, 2 * Y, pass_two, 0)
    send_last(0, dk_acc[0])
    finish(1, dv_out, 1.0)
    landed(d_recv, dq_in)
    dq = dq_acc[0]
    for t in range(3):
        dq = dq + dq_in[t].astype(F32)
    dq_out[...] = (dq * FACTOR).astype(BF16)
    finish(0, dk_out, FACTOR)

    left(a_send.at[0], gk.at[0, 0 : N - 1])
    left(a_send.at[1], gv.at[0, 0 : N - 1])
    left(a_send.at[2], gb.at[0 : N - 1])
    left(i_send, info.at[0:3])
    left(y_send.at[0], gq)
    left(y_send.at[1], gq.at[0:2])
    to_mate_k.wait_send()
    to_mate_v.wait_send()
    left(s_send.at[0], stats_in.at[0:3, 0:3])
    left(s_send.at[1], stats_in.at[0:3, 3:4])
    left(d_send, dq_in)
    for kind in (0, 1):
        core_copy(kind).wait_send()

        @pl.when(c != r)
        def _():
            left(p_send.at[kind], own_part.at[kind])

        @pl.when(c == r)
        def _():
            left(p_send.at[kind], own_part.at[kind, 0 : N - 1])


def local(*args):
    hbm = pl.BlockSpec(memory_space=pltpu.HBM)
    vmem = pl.BlockSpec(memory_space=pltpu.VMEM)
    V = pltpu.VMEM
    S = pltpu.SMEM
    dma = pltpu.SemaphoreType.DMA
    one = pltpu.SemaphoreType.DMA(())
    return pl.pallas_call(
        kernel,
        out_shape=(
            jax.ShapeDtypeStruct((DH, QN), BF16),
            jax.ShapeDtypeStruct((DH, 2 * BLK), BF16),
            jax.ShapeDtypeStruct((DH, 2 * BLK), BF16),
        ),
        in_specs=[hbm] * 8,
        out_specs=(vmem,) * 3,
        scratch_shapes=[
            S((N,), F32), S((4,), jnp.int32), S((2,), jnp.int32), V((N, QN), F32),
            V((2, N, SH, DH), BF16), V((2, N, SH, DH), BF16), V((N, 1, DH), F32), V((1, DH), F32),
            V((Y, QN, DH), BF16), V((Y, QN, DH), BF16), V((Y, 8, DH), F32),
            V((2, DH, KN), BF16), V((2, Y, KN, QN), F32), V((2, Y, KN, QN), F32), V((2, Y, KN, QN), BF16), V((KN, QN), BF16),
            V((KN, DH), F32), V((2, KN, DH), F32), V((Y, DH, QN), F32), V((2, Y, 8, DH), F32), V((Y, Y, 8, DH), F32), V((Y, 8, QN), F32),
            V((2, KN, DH), BF16), V((2, KN, DH), BF16), V((Y, DH, QN), BF16), V((3, DH, QN), BF16),
            V((2, N, SH, DH), BF16), V((2, N, SH, DH), BF16),
            dma((8,)), dma((3,)), dma((3,)), dma((2,)), dma((2,)), dma((2,)), dma((2, 3)), one, one, dma((2,)), dma((2,)),
            dma((2,)), dma((2,)), one, one, dma((2,)), dma((2,)),
        ],
        compiler_params=pltpu.CompilerParams(
            collective_id=0, has_side_effects=True, vmem_limit_bytes=48 * 1024 * 1024
        ),
    )(*[pltpu.with_memory_space_constraint(a, pltpu.HBM) for a in args])


def solution(mesh):
    in_specs = (
        P("row", None), P("col", None), P("col", None), P("row", None),
        P(None, "row"), P(), P("row"), P("col"),
    )
    out_specs = (P("col", "row"), P("row", "col"), P("row", "col"))
    return jax.shard_map(local, mesh=mesh, in_specs=in_specs, out_specs=out_specs, check_vma=False)
```

```python
import math

import jax
import jax.numpy as jnp
from jax import lax
from jax.experimental import pallas as pl
from jax.experimental.pallas import tpu as pltpu
from jax.sharding import PartitionSpec as P

MESH = pl.DeviceIdType.MESH
DH = 128
BLK = 128
QN = 512
N = 16
SH = 32
KN = N * SH
Y = 4
F32 = jnp.float32
BF16 = jnp.bfloat16
FACTOR = 1.0 / math.sqrt(DH)


def dot(a, b):
    return jnp.dot(a, b, preferred_element_type=F32)


def dot_nt(a, b):
    return lax.dot_general(a, b, (((1,), (1,)), ((), ())), preferred_element_type=F32)


def place(t):
    return t + t // 2 - 2 * (t // 3)


def kernel(
    queries, keys, values, out_grad, tau_in, alpha_in, query_blocks_in, key_blocks_in,
    dq_out, dk_out, dv_out,
    alpha, query_blocks, key_blocks, tau,
    gk, gv, gb, gb_send,
    gq, gg, info,
    kt, w_all, dp_all, probs, dv_acc, dk_acc, dq_own, stats, stats_in, shifts,
    core_out, core_in, dq_send, dq_in, own_part, row_part,
    in_sem, a_send, a_recv, x_send, x_recv, y_send, y_recv, i_send, i_recv, s_send, s_recv,
    c_send, c_recv, d_send, d_recv, p_send, p_recv, ready,
):
    r = lax.axis_index("row")
    c = lax.axis_index("col")
    y = r // 4
    xh = (r // 2) % 2
    core = r % 2
    other = 1 - core
    share = y * 2 + core

    def row_of(yy, cc):
        return yy * 4 + xh * 2 + cc

    mate = row_of(y, other)

    def send(src, dst, ssem, rsem, row, col):
        return pltpu.make_async_remote_copy(
            src_ref=src, dst_ref=dst, send_sem=ssem, recv_sem=rsem,
            device_id=(row, col), device_id_type=MESH,
        )

    def landed(sem, ref):
        send(ref, ref, in_sem.at[0], sem, mate, c).wait_recv()

    def left(sem, ref):
        send(ref, ref, sem, in_sem.at[0], mate, c).wait_send()

    barrier = pltpu.get_barrier_semaphore()

    def greet(row, col):
        pl.semaphore_signal(barrier, inc=1, device_id=(row, col), device_id_type=MESH)

    far_first = sorted(range(1, N), key=lambda j: -min(j, N - j))
    across = y * 4 + (1 - xh) * 2 + core
    for j in far_first:
        greet(r, (c + j) % N)
    greet(across, c)
    for j in range(1, Y):
        greet(row_of((y + j) % Y, core), c)
    greet(mate, c)

    key_rows = pl.ds(pl.multiple_of(share * SH, SH), SH)

    def head(h):
        return pl.ds(pl.multiple_of(h * DH, DH), DH)

    loads = [
        pltpu.make_async_copy(key_blocks_in, key_blocks, in_sem.at[0]),
        pltpu.make_async_copy(query_blocks_in, query_blocks, in_sem.at[1]),
        pltpu.make_async_copy(alpha_in, alpha, in_sem.at[2]),
        pltpu.make_async_copy(tau_in, tau, in_sem.at[3]),
        pltpu.make_async_copy(queries.at[:, head(c)], gq.at[y], in_sem.at[4]),
        pltpu.make_async_copy(out_grad.at[:, head(c)], gg.at[y], in_sem.at[5]),
        pltpu.make_async_copy(keys.at[key_rows, head(c)], gk.at[0, c], in_sem.at[6]),
        pltpu.make_async_copy(values.at[key_rows, head(c)], gv.at[0, c], in_sem.at[7]),
    ]
    for load in loads:
        load.start()
    pl.semaphore_wait(barrier, N + Y)
    pl.semaphore_signal(ready, inc=1, device_id=(across, c), device_id_type=MESH)

    def to_columns(kind):
        for j in far_first:
            peer = (c + j) % N
            src, dst = (
                (keys.at[key_rows, head(peer)], gk.at[0, c]),
                (values.at[key_rows, head(peer)], gv.at[0, c]),
                (gb_send, gb.at[c]),
            )[kind]
            send(src, dst, a_send.at[kind], a_recv.at[kind], r, peer).start()

    own = (queries, out_grad)
    group = (gq, gg)
    HALF = (pl.ds(0, QN // 2), pl.ds(QN // 2, QN // 2))

    def along_y(way, stage):
        step = 1 if way == 0 else 3
        part = HALF[way] if stage != 1 else HALF[1 - way]
        m = y if stage < 2 else (y + 4 - step) % Y
        for kind in (0, 1):
            dst = group[kind].at[m, part]
            src = own[kind].at[part, head(c)] if stage < 2 else dst
            send(
                src, dst, y_send.at[stage // 2], y_recv.at[way, stage], row_of((y + step) % Y, core), c
            ).start()

    def from_y(way, stage):
        landed(y_recv.at[way, stage], gq.at[0])

    to_columns(0)
    for way in (0, 1):
        along_y(way, 0)
    for load in loads[:4]:
        load.wait()
    base = (key_blocks[share // 4] * BLK + (share % 4) * SH).astype(F32)
    gb_send[...] = jnp.full((1, DH), base)
    gb[c] = gb_send[...]
    line = tau[pl.ds(c, 1), :]
    for i in range(4):
        info[y, i : i + 1, :] = line[:, i * DH : (i + 1) * DH]
        info[y, 4 + i : 5 + i, :] = jnp.full((1, DH), query_blocks[i] * BLK).astype(F32)
    to_columns(2)
    for j in range(1, Y):
        send(info.at[y], info.at[y], i_send, i_recv, row_of((y + j) % Y, core), c).start()
    to_columns(1)
    for way in (0, 1):
        along_y(way, 1)

    dk_acc[...] = jnp.zeros_like(dk_acc)
    excess = jnp.full((8, QN), alpha[c]) - 1.0
    scale = excess * FACTOR
    power = (1.0 - excess) / excess * (1.0 / math.log(2.0))
    lane = lax.broadcasted_iota(jnp.int32, (8, QN), 1) % BLK
    row8 = lax.broadcasted_iota(jnp.int32, (8, QN), 0)
    ahead = (lane - row8).astype(F32)

    def wide(tile, lo):
        line = jnp.concatenate([tile[lo + i : lo + i + 1, :] for i in range(4)], axis=1)
        return jnp.broadcast_to(line, (8, QN))

    for load in loads[4:]:
        load.wait()
    for way in (0, 1):
        from_y(way, 0)
        along_y(way, 2)
    landed(i_recv, info.at[0:3])
    landed(a_recv.at[0], gk.at[0, 0 : N - 1])
    to_mate_k = send(gk.at[0], gk.at[1], x_send.at[0], x_recv.at[0], mate, c)
    to_mate_v = send(gv.at[0], gv.at[1], x_send.at[1], x_recv.at[1], mate, c)
    pl.semaphore_wait(ready, 1)
    to_mate_k.start()
    kt[0] = gk[0].reshape(KN, DH).T
    landed(a_recv.at[2], gb.at[0 : N - 1])

    def lines(total):
        total = jnp.sum(total, axis=0, keepdims=True)
        return jnp.concatenate([total[:, i * DH : (i + 1) * DH] for i in range(4)], axis=0)

    def member(t):
        return (y + 4 - place(t)) % Y

    def weigh(h, t):
        m = member(t)
        scores = dot_nt(gk[h].reshape(KN, DH), gq[m])
        tile = info[m]
        shift_in = wide(tile, 0) * excess
        query = wide(tile, 4) + ahead - (h * SH * (other - core)).astype(F32)
        m_sum = jnp.zeros((8, QN), F32)
        for j in range(N):
            b = jnp.broadcast_to(jnp.concatenate([gb[j]] * (QN // DH), axis=1), (8, QN))
            for i in range(SH // 16):
                pair = []
                for lo in (j * SH + i * 16, j * SH + i * 16 + 8):
                    x = scores[lo : lo + 8] * scale - shift_in
                    x = jnp.where(b + (lo - j * SH) <= query, jnp.maximum(x, 0.0), 0.0)
                    w = jnp.exp2(jnp.log(x) * power)
                    w_all[h, t, lo : lo + 8, :] = w
                    pair.append(w * x)
                    m_sum = m_sum + w
                probs[h, t, lo - 8 : lo + 8, :] = jnp.concatenate(pair, axis=0).astype(BF16)
        stats[h, t, 4:8, :] = lines(m_sum)

    def match(h, t):
        dp = dot_nt(gv[h].reshape(KN, DH), gg[member(t)])
        dp_all[h, t] = dp
        t_sum = jnp.zeros((8, QN), F32)
        for lo in range(0, KN, 8):
            t_sum = t_sum + w_all[h, t, lo : lo + 8, :] * dp[lo : lo + 8]
        stats[h, t, 0:4, :] = lines(t_sum)

    def sums_to_y(lo, hi):
        stats[0, lo:hi] = stats[0, lo:hi] + stats[1, lo:hi]
        for j in range(1, Y):
            send(
                stats.at[0, lo:hi], stats_in.at[y, lo:hi], s_send.at[lo // 3], s_recv.at[lo // 3],
                row_of((y + j) % Y, core), c,
            ).start()

    def weigh_and_match(h, t):
        m = member(t)
        scores = dot_nt(gk[h].reshape(KN, DH), gq[m])
        dp = dot_nt(gv[h].reshape(KN, DH), gg[m])
        dp_all[h, t] = dp
        tile = info[m]
        shift_in = wide(tile, 0) * excess
        query = wide(tile, 4) + ahead - (h * SH * (other - core)).astype(F32)
        t_sum = jnp.zeros((8, QN), F32)
        m_sum = jnp.zeros((8, QN), F32)
        for j in range(N):
            b = jnp.broadcast_to(jnp.concatenate([gb[j]] * (QN // DH), axis=1), (8, QN))
            for i in range(SH // 16):
                pair = []
                for lo in (j * SH + i * 16, j * SH + i * 16 + 8):
                    x = scores[lo : lo + 8] * scale - shift_in
                    x = jnp.where(b + (lo - j * SH) <= query, jnp.maximum(x, 0.0), 0.0)
                    w = jnp.exp2(jnp.log(x) * power)
                    w_all[h, t, lo : lo + 8, :] = w
                    pair.append(w * x)
                    t_sum = t_sum + w * dp[lo : lo + 8]
                    m_sum = m_sum + w
                probs[h, t, lo - 8 : lo + 8, :] = jnp.concatenate(pair, axis=0).astype(BF16)
        stats[h, t, 0:4, :] = lines(t_sum)
        stats[h, t, 4:8, :] = lines(m_sum)

    def weigh_early(i, carry):
        for way in (0, 1):

            @pl.when(i == 1 + way)
            def _():
                from_y(way, 1)

        @pl.when(i == 3)
        def _():
            landed(x_recv.at[0], gk.at[1])

        @pl.when(i == 4)
        def _():
            landed(a_recv.at[1], gv.at[0, 0 : N - 1])
            to_mate_v.start()

        weigh(i // 3, i % 3)
        return carry

    def match_own(i, carry):
        match(0, i)
        return carry

    def match_other(i, carry):
        match(1, i)
        return carry

    def rest(i, carry):
        @pl.when(i == 1)
        def _():
            landed(x_recv.at[1], gv.at[1])
            lax.fori_loop(0, 2, match_other, 0)

        weigh_and_match(1 - (2 - i) // 2, 3 - i % 2)

        @pl.when(i == 1)
        def _():
            sums_to_y(0, 3)

        return carry

    lax.fori_loop(0, 5, weigh_early, 0)
    lax.fori_loop(0, 3, match_own, 0)
    for way in (0, 1):
        from_y(way, 2)
    lax.fori_loop(0, 3, rest, 0)
    sums_to_y(3, 4)
    kt[1] = gk[1].reshape(KN, DH).T

    def core_copy(kind):
        return send(core_out.at[kind], core_in.at[kind], c_send.at[kind], c_recv.at[kind], mate, c)

    def add_values(i, carry):
        h = 1 - i // Y
        t = i % Y

        @pl.when(t == 0)
        def _():
            dv_acc[...] = jnp.zeros_like(dv_acc)

        dv_acc[...] += dot(probs[h, t], gg[member(t)])

        @pl.when(i == Y - 1)
        def _():
            core_out[1] = dv_acc[...].astype(BF16)
            core_copy(1).start()

        return carry

    lax.fori_loop(0, 2 * Y, add_values, 0, unroll=2)

    def send_last(kind, total):
        landed(c_recv.at[kind], core_in.at[kind])
        total = total + core_in[kind].astype(F32)
        own_part[kind] = total.astype(BF16).reshape(N, SH, DH)

        def one(j):
            peer = (c + j) % N
            send(
                own_part.at[kind, peer], row_part.at[kind, r], p_send.at[kind], p_recv.at[kind], c, peer
            ).start()

        for j in range(1, N):
            one(j)

        @pl.when(c != r)
        def _():
            one(0)

        @pl.when(c == r)
        def _():
            row_part[kind, r] = own_part[kind, c]

    def finish(kind, out, factor):
        @pl.when(c != r)
        def _():
            landed(p_recv.at[kind], row_part.at[kind])

        @pl.when(c == r)
        def _():
            landed(p_recv.at[kind], row_part.at[kind, 0 : N - 1])

        pairs = row_part[kind].astype(F32).reshape(4, 2, 2, SH, DH)
        pairs = (pairs[:, 0] + pairs[:, 1]).reshape(8 * SH, DH)
        out[...] = (pairs.T * factor).astype(BF16)

    landed(s_recv.at[0], stats_in.at[0:3, 0:3])
    landed(s_recv.at[1], stats_in.at[0:3, 3:4])
    stats_in[y] = stats[0]

    def one_shift(t, carry):
        m = member(t)
        total = jnp.zeros((8, DH), F32)
        for src in range(Y):
            total = total + stats_in[src, place((src + 4 - m) % Y)]
        shift = total[0:4] / jnp.maximum(total[4:8], 1.0)
        shifts[t] = wide(shift, 0)
        return carry

    lax.fori_loop(0, Y, one_shift, 0)

    def score_grad(h, t):
        row_shift = shifts[t]
        for lo in range(0, KN, 16):
            pair = [w_all[h, t, i : i + 8, :] * (dp_all[h, t, i : i + 8, :] - row_shift) for i in (lo, lo + 8)]
            probs[h, t, lo : lo + 16, :] = jnp.concatenate(pair, axis=0).astype(BF16)
        ds = probs[h, t]
        dk_acc[h] += dot(ds, gq[member(t)])
        return ds

    def other_share(i, carry):
        score_grad(1, 3 - i)
        return carry

    def own_share(i, carry):
        t = 3 - i
        ds = score_grad(0, t)
        part = dot(kt[0], ds) + dot(kt[1], probs[1, t])

        @pl.when(t == 0)
        def _():
            dq_own[...] = part

        @pl.when(t > 0)
        def _():
            dq_send[t] = part.astype(BF16)

        for tt in (3, 2, 1):

            @pl.when(t == tt)
            def _():
                send(dq_send.at[tt], dq_in.at[tt - 1], d_send, d_recv, row_of(member(tt), core), c).start()

        @pl.when(i == 0)
        def _():
            send_last(1, dv_acc[...])

        return carry

    lax.fori_loop(0, Y, other_share, 0, unroll=2)
    core_out[0] = dk_acc[1].astype(BF16)
    core_copy(0).start()
    lax.fori_loop(0, Y, own_share, 0, unroll=2)
    send_last(0, dk_acc[0])
    finish(1, dv_out, 1.0)
    landed(d_recv, dq_in)
    dq = dq_own[...]
    for t in range(3):
        dq = dq + dq_in[t].astype(F32)
    dq_out[...] = (dq * FACTOR).astype(BF16)
    finish(0, dk_out, FACTOR)

    left(a_send.at[0], gk.at[0, 0 : N - 1])
    left(a_send.at[1], gv.at[0, 0 : N - 1])
    left(a_send.at[2], gb.at[0 : N - 1])
    left(i_send, info.at[0:3])
    left(y_send.at[0], gq)
    left(y_send.at[1], gq.at[0:2])
    to_mate_k.wait_send()
    to_mate_v.wait_send()
    left(s_send.at[0], stats_in.at[0:3, 0:3])
    left(s_send.at[1], stats_in.at[0:3, 3:4])
    left(d_send, dq_in)
    for kind in (0, 1):
        core_copy(kind).wait_send()

        @pl.when(c != r)
        def _():
            left(p_send.at[kind], own_part.at[kind])

        @pl.when(c == r)
        def _():
            left(p_send.at[kind], own_part.at[kind, 0 : N - 1])


def local(*args):
    hbm = pl.BlockSpec(memory_space=pltpu.HBM)
    vmem = pl.BlockSpec(memory_space=pltpu.VMEM)
    V = pltpu.VMEM
    S = pltpu.SMEM
    dma = pltpu.SemaphoreType.DMA
    one = pltpu.SemaphoreType.DMA(())
    return pl.pallas_call(
        kernel,
        out_shape=(
            jax.ShapeDtypeStruct((DH, QN), BF16),
            jax.ShapeDtypeStruct((DH, 2 * BLK), BF16),
            jax.ShapeDtypeStruct((DH, 2 * BLK), BF16),
        ),
        in_specs=[hbm] * 8,
        out_specs=(vmem,) * 3,
        scratch_shapes=[
            S((N,), F32), S((4,), jnp.int32), S((2,), jnp.int32), V((N, QN), F32),
            V((2, N, SH, DH), BF16), V((2, N, SH, DH), BF16), V((N, 1, DH), F32), V((1, DH), F32),
            V((Y, QN, DH), BF16), V((Y, QN, DH), BF16), V((Y, 8, DH), F32),
            V((2, DH, KN), BF16), V((2, Y, KN, QN), F32), V((2, Y, KN, QN), F32), V((2, Y, KN, QN), BF16),
            V((KN, DH), F32), V((2, KN, DH), F32), V((DH, QN), F32), V((2, Y, 8, DH), F32), V((Y, Y, 8, DH), F32), V((Y, 8, QN), F32),
            V((2, KN, DH), BF16), V((2, KN, DH), BF16), V((Y, DH, QN), BF16), V((3, DH, QN), BF16),
            V((2, N, SH, DH), BF16), V((2, N, SH, DH), BF16),
            dma((8,)), dma((3,)), dma((3,)), dma((2,)), dma((2,)), dma((2,)), dma((2, 3)), one, one, dma((2,)), dma((2,)),
            dma((2,)), dma((2,)), one, one, dma((2,)), dma((2,)), pltpu.SemaphoreType.REGULAR,
        ],
        compiler_params=pltpu.CompilerParams(
            collective_id=0, has_side_effects=True, vmem_limit_bytes=48 * 1024 * 1024
        ),
    )(*[pltpu.with_memory_space_constraint(a, pltpu.HBM) for a in args])


def solution(mesh):
    in_specs = (
        P("row", None), P("col", None), P("col", None), P("row", None),
        P(None, "row"), P(), P("row"), P("col"),
    )
    out_specs = (P("col", "row"), P("row", "col"), P("row", "col"))
    return jax.shard_map(local, mesh=mesh, in_specs=in_specs, out_specs=out_specs, check_vma=False)
```

```python
import math

import jax
import jax.numpy as jnp
from jax import lax
from jax.experimental import pallas as pl
from jax.experimental.pallas import tpu as pltpu
from jax.sharding import PartitionSpec as P

MESH = pl.DeviceIdType.MESH
DH = 128
BLK = 128
QN = 512
N = 16
SH = 32
KN = N * SH
Y = 4
F32 = jnp.float32
BF16 = jnp.bfloat16
FACTOR = 1.0 / math.sqrt(DH)


def dot(a, b):
    return jnp.dot(a, b, preferred_element_type=F32)


def dot_nt(a, b):
    return lax.dot_general(a, b, (((1,), (1,)), ((), ())), preferred_element_type=F32)


def place(t):
    return t + t // 2 - 2 * (t // 3)


def kernel(
    queries, keys, values, out_grad, tau_in, alpha_in, query_blocks_in, key_blocks_in,
    dq_out, dk_out, dv_out,
    alpha, query_blocks, key_blocks, tau,
    gk, gv, gb, gb_send,
    gq, gg, info,
    kt, w_all, dp_all, probs, dv_acc, dk_acc, dq_own, stats, stats_in, shifts,
    core_out, core_in, dq_send, dq_in, own_part, row_part,
    in_sem, a_send, a_recv, x_send, x_recv, y_send, y_recv, i_send, i_recv, s_send, s_recv,
    c_send, c_recv, d_send, d_recv, p_send, p_recv, ready,
):
    r = lax.axis_index("row")
    c = lax.axis_index("col")
    y = r // 4
    xh = (r // 2) % 2
    core = r % 2
    other = 1 - core
    share = y * 2 + core

    def row_of(yy, cc):
        return yy * 4 + xh * 2 + cc

    mate = row_of(y, other)

    def send(src, dst, ssem, rsem, row, col):
        return pltpu.make_async_remote_copy(
            src_ref=src, dst_ref=dst, send_sem=ssem, recv_sem=rsem,
            device_id=(row, col), device_id_type=MESH,
        )

    def landed(sem, ref):
        send(ref, ref, in_sem.at[0], sem, mate, c).wait_recv()

    def left(sem, ref):
        send(ref, ref, sem, in_sem.at[0], mate, c).wait_send()

    barrier = pltpu.get_barrier_semaphore()

    def greet(row, col):
        pl.semaphore_signal(barrier, inc=1, device_id=(row, col), device_id_type=MESH)

    far_first = sorted(range(1, N), key=lambda j: -min(j, N - j))
    across = y * 4 + (1 - xh) * 2 + core
    for j in far_first:
        greet(r, (c + j) % N)
    greet(across, c)
    for j in range(1, Y):
        greet(row_of((y + j) % Y, core), c)
    greet(mate, c)

    key_rows = pl.ds(pl.multiple_of(share * SH, SH), SH)

    def head(h):
        return pl.ds(pl.multiple_of(h * DH, DH), DH)

    loads = [
        pltpu.make_async_copy(key_blocks_in, key_blocks, in_sem.at[0]),
        pltpu.make_async_copy(query_blocks_in, query_blocks, in_sem.at[1]),
        pltpu.make_async_copy(alpha_in, alpha, in_sem.at[2]),
        pltpu.make_async_copy(tau_in, tau, in_sem.at[3]),
        pltpu.make_async_copy(queries.at[:, head(c)], gq.at[y], in_sem.at[4]),
        pltpu.make_async_copy(out_grad.at[:, head(c)], gg.at[y], in_sem.at[5]),
        pltpu.make_async_copy(keys.at[key_rows, head(c)], gk.at[0, c], in_sem.at[6]),
        pltpu.make_async_copy(values.at[key_rows, head(c)], gv.at[0, c], in_sem.at[7]),
    ]
    for load in loads:
        load.start()
    pl.semaphore_wait(barrier, N + Y)
    pl.semaphore_signal(ready, inc=1, device_id=(across, c), device_id_type=MESH)

    def to_columns(kind):
        for j in far_first:
            peer = (c + j) % N
            src, dst = (
                (keys.at[key_rows, head(peer)], gk.at[0, c]),
                (values.at[key_rows, head(peer)], gv.at[0, c]),
                (gb_send, gb.at[c]),
            )[kind]
            send(src, dst, a_send.at[kind], a_recv.at[kind], r, peer).start()

    own = (queries, out_grad)
    group = (gq, gg)
    HALF = (pl.ds(0, QN // 2), pl.ds(QN // 2, QN // 2))

    def along_y(way, stage):
        step = 1 if way == 0 else 3
        part = HALF[way] if stage != 1 else HALF[1 - way]
        m = y if stage < 2 else (y + 4 - step) % Y
        for kind in (0, 1):
            dst = group[kind].at[m, part]
            src = own[kind].at[part, head(c)] if stage < 2 else dst
            send(
                src, dst, y_send.at[stage // 2], y_recv.at[way, stage], row_of((y + step) % Y, core), c
            ).start()

    def from_y(way, stage):
        landed(y_recv.at[way, stage], gq.at[0])

    to_columns(0)
    for way in (0, 1):
        along_y(way, 0)
    for load in loads[:4]:
        load.wait()
    base = (key_blocks[share // 4] * BLK + (share % 4) * SH).astype(F32)
    gb_send[...] = jnp.full((1, DH), base)
    gb[c] = gb_send[...]
    line = tau[pl.ds(c, 1), :]
    for i in range(4):
        info[y, i : i + 1, :] = line[:, i * DH : (i + 1) * DH]
        info[y, 4 + i : 5 + i, :] = jnp.full((1, DH), query_blocks[i] * BLK).astype(F32)
    to_columns(2)
    for j in range(1, Y):
        send(info.at[y], info.at[y], i_send, i_recv, row_of((y + j) % Y, core), c).start()
    to_columns(1)
    for way in (0, 1):
        along_y(way, 1)

    dk_acc[...] = jnp.zeros_like(dk_acc)
    excess = jnp.full((8, QN), alpha[c]) - 1.0
    scale = excess * FACTOR
    power = (1.0 - excess) / excess * (1.0 / math.log(2.0))
    lane = lax.broadcasted_iota(jnp.int32, (8, QN), 1) % BLK
    row8 = lax.broadcasted_iota(jnp.int32, (8, QN), 0)
    ahead = (lane - row8).astype(F32)

    def wide(tile, lo):
        line = jnp.concatenate([tile[lo + i : lo + i + 1, :] for i in range(4)], axis=1)
        return jnp.broadcast_to(line, (8, QN))

    for load in loads[4:]:
        load.wait()
    for way in (0, 1):
        from_y(way, 0)
        along_y(way, 2)
    landed(i_recv, info.at[0:3])
    landed(a_recv.at[0], gk.at[0, 0 : N - 1])
    to_mate_k = send(gk.at[0], gk.at[1], x_send.at[0], x_recv.at[0], mate, c)
    to_mate_v = send(gv.at[0], gv.at[1], x_send.at[1], x_recv.at[1], mate, c)
    pl.semaphore_wait(ready, 1)
    to_mate_k.start()
    kt[0] = gk[0].reshape(KN, DH).T
    landed(a_recv.at[2], gb.at[0 : N - 1])

    def lines(total):
        total = jnp.sum(total, axis=0, keepdims=True)
        return jnp.concatenate([total[:, i * DH : (i + 1) * DH] for i in range(4)], axis=0)

    def member(t):
        return (y + 4 - place(t)) % Y

    def weigh(h, t):
        m = member(t)
        scores = dot_nt(gk[h].reshape(KN, DH), gq[m])
        tile = info[m]
        shift_in = wide(tile, 0) * excess
        query = wide(tile, 4) + ahead - (h * SH * (other - core)).astype(F32)
        m_sum = jnp.zeros((8, QN), F32)
        for j in range(N):
            b = jnp.broadcast_to(jnp.concatenate([gb[j]] * (QN // DH), axis=1), (8, QN))
            for i in range(SH // 16):
                pair = []
                for lo in (j * SH + i * 16, j * SH + i * 16 + 8):
                    x = scores[lo : lo + 8] * scale - shift_in
                    x = jnp.where(b + (lo - j * SH) <= query, jnp.maximum(x, 0.0), 0.0)
                    w = jnp.exp2(jnp.log(x) * power)
                    w_all[h, t, lo : lo + 8, :] = w
                    pair.append(w * x)
                    m_sum = m_sum + w
                probs[h, t, lo - 8 : lo + 8, :] = jnp.concatenate(pair, axis=0).astype(BF16)
        stats[h, t, 4:8, :] = lines(m_sum)

    def match(h, t):
        dp = dot_nt(gv[h].reshape(KN, DH), gg[member(t)])
        dp_all[h, t] = dp
        t_sum = jnp.zeros((8, QN), F32)
        for lo in range(0, KN, 8):
            t_sum = t_sum + w_all[h, t, lo : lo + 8, :] * dp[lo : lo + 8]
        stats[h, t, 0:4, :] = lines(t_sum)

    def sums_to_y(lo, hi):
        stats[0, lo:hi] = stats[0, lo:hi] + stats[1, lo:hi]
        for j in range(1, Y):
            send(
                stats.at[0, lo:hi], stats_in.at[y, lo:hi], s_send.at[lo // 3], s_recv.at[lo // 3],
                row_of((y + j) % Y, core), c,
            ).start()

    def weigh_and_match(h, t):
        m = member(t)
        scores = dot_nt(gk[h].reshape(KN, DH), gq[m])
        dp = dot_nt(gv[h].reshape(KN, DH), gg[m])
        dp_all[h, t] = dp
        tile = info[m]
        shift_in = wide(tile, 0) * excess
        query = wide(tile, 4) + ahead - (h * SH * (other - core)).astype(F32)
        t_sum = jnp.zeros((8, QN), F32)
        m_sum = jnp.zeros((8, QN), F32)
        for j in range(N):
            b = jnp.broadcast_to(jnp.concatenate([gb[j]] * (QN // DH), axis=1), (8, QN))
            for i in range(SH // 16):
                pair = []
                for lo in (j * SH + i * 16, j * SH + i * 16 + 8):
                    x = scores[lo : lo + 8] * scale - shift_in
                    x = jnp.where(b + (lo - j * SH) <= query, jnp.maximum(x, 0.0), 0.0)
                    w = jnp.exp2(jnp.log(x) * power)
                    w_all[h, t, lo : lo + 8, :] = w
                    pair.append(w * x)
                    t_sum = t_sum + w * dp[lo : lo + 8]
                    m_sum = m_sum + w
                probs[h, t, lo - 8 : lo + 8, :] = jnp.concatenate(pair, axis=0).astype(BF16)
        stats[h, t, 0:4, :] = lines(t_sum)
        stats[h, t, 4:8, :] = lines(m_sum)

    def weigh_early(i, carry):
        for way in (0, 1):

            @pl.when(i == 1 + way)
            def _():
                from_y(way, 1)

        @pl.when(i == 3)
        def _():
            landed(x_recv.at[0], gk.at[1])

        @pl.when(i == 4)
        def _():
            landed(a_recv.at[1], gv.at[0, 0 : N - 1])
            to_mate_v.start()

        weigh(i // 3, i % 3)
        return carry

    def match_own(i, carry):
        match(0, i)
        return carry

    def match_other(i, carry):
        match(1, i)
        return carry

    def rest(i, carry):
        @pl.when(i == 1)
        def _():
            landed(x_recv.at[1], gv.at[1])
            lax.fori_loop(0, 2, match_other, 0)

        weigh_and_match(1 - (2 - i) // 2, 3 - i % 2)

        @pl.when(i == 1)
        def _():
            sums_to_y(0, 3)

        return carry

    lax.fori_loop(0, 5, weigh_early, 0)
    lax.fori_loop(0, 3, match_own, 0)
    for way in (0, 1):
        from_y(way, 2)
    lax.fori_loop(0, 3, rest, 0)
    sums_to_y(3, 4)
    kt[1] = gk[1].reshape(KN, DH).T

    def core_copy(kind):
        return send(core_out.at[kind], core_in.at[kind], c_send.at[kind], c_recv.at[kind], mate, c)

    def add_values(i, carry):
        h = 1 - i // Y
        t = i % Y

        @pl.when(t == 0)
        def _():
            dv_acc[...] = jnp.zeros_like(dv_acc)

        dv_acc[...] += dot(probs[h, t], gg[member(t)])

        @pl.when(i == Y - 1)
        def _():
            core_out[1] = dv_acc[...].astype(BF16)
            core_copy(1).start()

        return carry

    lax.fori_loop(0, 2 * Y, add_values, 0, unroll=2)

    def send_last(kind, total):
        landed(c_recv.at[kind], core_in.at[kind])
        total = total + core_in[kind].astype(F32)
        own_part[kind] = total.astype(BF16).reshape(N, SH, DH)

        def one(j):
            peer = (c + j) % N
            send(
                own_part.at[kind, peer], row_part.at[kind, r], p_send.at[kind], p_recv.at[kind], c, peer
            ).start()

        for j in range(1, N):
            one(j)

        @pl.when(c != r)
        def _():
            one(0)

        @pl.when(c == r)
        def _():
            row_part[kind, r] = own_part[kind, c]

    def finish(kind, out, factor):
        @pl.when(c != r)
        def _():
            landed(p_recv.at[kind], row_part.at[kind])

        @pl.when(c == r)
        def _():
            landed(p_recv.at[kind], row_part.at[kind, 0 : N - 1])

        pairs = row_part[kind].astype(F32).reshape(4, 2, 2, SH, DH)
        pairs = (pairs[:, 0] + pairs[:, 1]).reshape(8 * SH, DH)
        out[...] = (pairs.T * factor).astype(BF16)

    landed(s_recv.at[0], stats_in.at[0:3, 0:3])
    landed(s_recv.at[1], stats_in.at[0:3, 3:4])
    stats_in[y] = stats[0]

    def one_shift(t, carry):
        m = member(t)
        total = jnp.zeros((8, DH), F32)
        for src in range(Y):
            total = total + stats_in[src, place((src + 4 - m) % Y)]
        shift = total[0:4] / jnp.maximum(total[4:8], 1.0)
        shifts[t] = wide(shift, 0)
        return carry

    lax.fori_loop(0, Y, one_shift, 0)

    def score_grad(h, t):
        row_shift = shifts[t]
        for lo in range(0, KN, 16):
            pair = [w_all[h, t, i : i + 8, :] * (dp_all[h, t, i : i + 8, :] - row_shift) for i in (lo, lo + 8)]
            probs[h, t, lo : lo + 16, :] = jnp.concatenate(pair, axis=0).astype(BF16)
        ds = probs[h, t]
        dk_acc[h] += dot(ds, gq[member(t)])
        return ds

    def other_share(i, carry):
        score_grad(1, 3 - i)
        return carry

    def own_share(i, carry):
        t = 3 - i
        ds = score_grad(0, t)
        part = dot(kt[0], ds) + dot(kt[1], probs[1, t])

        @pl.when(t == 0)
        def _():
            dq_own[...] = part

        @pl.when(t > 0)
        def _():
            dq_send[t] = part.astype(BF16)

        for tt in (3, 2, 1):

            @pl.when(t == tt)
            def _():
                send(dq_send.at[tt], dq_in.at[tt - 1], d_send, d_recv, row_of(member(tt), core), c).start()

        @pl.when(i == 0)
        def _():
            send_last(1, dv_acc[...])

        return carry

    lax.fori_loop(0, Y, other_share, 0, unroll=2)
    core_out[0] = dk_acc[1].astype(BF16)
    core_copy(0).start()
    lax.fori_loop(0, Y, own_share, 0, unroll=2)
    send_last(0, dk_acc[0])
    finish(1, dv_out, 1.0)
    landed(d_recv, dq_in)
    dq = dq_own[...]
    for t in range(3):
        dq = dq + dq_in[t].astype(F32)
    dq_out[...] = (dq * FACTOR).astype(BF16)
    finish(0, dk_out, FACTOR)

    left(a_send.at[0], gk.at[0, 0 : N - 1])
    left(a_send.at[1], gv.at[0, 0 : N - 1])
    left(a_send.at[2], gb.at[0 : N - 1])
    left(i_send, info.at[0:3])
    left(y_send.at[0], gq)
    left(y_send.at[1], gq.at[0:2])
    to_mate_k.wait_send()
    to_mate_v.wait_send()
    left(s_send.at[0], stats_in.at[0:3, 0:3])
    left(s_send.at[1], stats_in.at[0:3, 3:4])
    left(d_send, dq_in)
    for kind in (0, 1):
        core_copy(kind).wait_send()

        @pl.when(c != r)
        def _():
            left(p_send.at[kind], own_part.at[kind])

        @pl.when(c == r)
        def _():
            left(p_send.at[kind], own_part.at[kind, 0 : N - 1])


def store(dq, dk, dv, dq_out, dk_out, dv_out, sem):
    copies = [
        pltpu.make_async_copy(src, dst, sem.at[i])
        for i, (src, dst) in enumerate(((dq, dq_out), (dk, dk_out), (dv, dv_out)))
    ]
    for copy in copies:
        copy.start()
    for copy in copies:
        copy.wait()


def local(*args):
    hbm = pl.BlockSpec(memory_space=pltpu.HBM)
    vmem = pl.BlockSpec(memory_space=pltpu.VMEM)
    V = pltpu.VMEM
    S = pltpu.SMEM
    dma = pltpu.SemaphoreType.DMA
    one = pltpu.SemaphoreType.DMA(())
    shapes = (
        jax.ShapeDtypeStruct((DH, QN), BF16),
        jax.ShapeDtypeStruct((DH, 2 * BLK), BF16),
        jax.ShapeDtypeStruct((DH, 2 * BLK), BF16),
    )
    grads = pl.pallas_call(
        kernel,
        out_shape=shapes,
        in_specs=[hbm] * 8,
        out_specs=(vmem,) * 3,
        scratch_shapes=[
            S((N,), F32), S((4,), jnp.int32), S((2,), jnp.int32), V((N, QN), F32),
            V((2, N, SH, DH), BF16), V((2, N, SH, DH), BF16), V((N, 1, DH), F32), V((1, DH), F32),
            V((Y, QN, DH), BF16), V((Y, QN, DH), BF16), V((Y, 8, DH), F32),
            V((2, DH, KN), BF16), V((2, Y, KN, QN), F32), V((2, Y, KN, QN), F32), V((2, Y, KN, QN), BF16),
            V((KN, DH), F32), V((2, KN, DH), F32), V((DH, QN), F32), V((2, Y, 8, DH), F32), V((Y, Y, 8, DH), F32), V((Y, 8, QN), F32),
            V((2, KN, DH), BF16), V((2, KN, DH), BF16), V((Y, DH, QN), BF16), V((3, DH, QN), BF16),
            V((2, N, SH, DH), BF16), V((2, N, SH, DH), BF16),
            dma((8,)), dma((3,)), dma((3,)), dma((2,)), dma((2,)), dma((2,)), dma((2, 3)), one, one, dma((2,)), dma((2,)),
            dma((2,)), dma((2,)), one, one, dma((2,)), dma((2,)), pltpu.SemaphoreType.REGULAR,
        ],
        compiler_params=pltpu.CompilerParams(
            collective_id=0, has_side_effects=True, vmem_limit_bytes=48 * 1024 * 1024
        ),
    )(*[pltpu.with_memory_space_constraint(a, pltpu.HBM) for a in args])

    return pl.pallas_call(
        store,
        out_shape=shapes,
        in_specs=[vmem] * 3,
        out_specs=(hbm,) * 3,
        scratch_shapes=[dma((3,))],
    )(*[pltpu.with_memory_space_constraint(g, pltpu.VMEM) for g in grads])

def solution(mesh):
    in_specs = (
        P("row", None), P("col", None), P("col", None), P("row", None),
        P(None, "row"), P(), P("row"), P("col"),
    )
    out_specs = (P("col", "row"), P("row", "col"), P("row", "col"))
    return jax.shard_map(local, mesh=mesh, in_specs=in_specs, out_specs=out_specs, check_vma=False)
```

```python
import math

import jax
import jax.numpy as jnp
from jax import lax
from jax.experimental import pallas as pl
from jax.experimental.pallas import tpu as pltpu
from jax.sharding import PartitionSpec as P

MESH = pl.DeviceIdType.MESH
DH = 128
BLK = 128
QN = 512
N = 16
SH = 32
KN = N * SH
Y = 4
F32 = jnp.float32
BF16 = jnp.bfloat16
FACTOR = 1.0 / math.sqrt(DH)


def dot(a, b):
    return jnp.dot(a, b, preferred_element_type=F32)


def dot_nt(a, b):
    return lax.dot_general(a, b, (((1,), (1,)), ((), ())), preferred_element_type=F32)


def place(t):
    return t + t // 2 - 2 * (t // 3)


def kernel(
    queries, keys, values, out_grad, tau_in, alpha_in, query_blocks_in, key_blocks_in,
    dq_out, dk_out, dv_out,
    alpha, query_blocks, key_blocks, tau,
    gk, gv, gb, gb_send,
    gq, gg, info,
    kt, w_all, dp_all, probs, dv_acc, dk_acc, dq_own, stats, stats_in, shifts,
    core_out, core_in, dq_send, dq_in, own_part, row_part,
    in_sem, a_send, a_recv, x_send, x_recv, y_send, y_recv, i_send, i_recv, s_send, s_recv,
    c_send, c_recv, d_send, d_recv, p_send, p_recv, ready,
):
    r = lax.axis_index("row")
    c = lax.axis_index("col")
    y = r // 4
    xh = (r // 2) % 2
    core = r % 2
    other = 1 - core
    share = y * 2 + core

    def row_of(yy, cc):
        return yy * 4 + xh * 2 + cc

    mate = row_of(y, other)

    def send(src, dst, ssem, rsem, row, col):
        return pltpu.make_async_remote_copy(
            src_ref=src, dst_ref=dst, send_sem=ssem, recv_sem=rsem,
            device_id=(row, col), device_id_type=MESH,
        )

    def landed(sem, ref):
        send(ref, ref, in_sem.at[0], sem, mate, c).wait_recv()

    def left(sem, ref):
        send(ref, ref, sem, in_sem.at[0], mate, c).wait_send()

    barrier = pltpu.get_barrier_semaphore()

    def greet(row, col):
        pl.semaphore_signal(barrier, inc=1, device_id=(row, col), device_id_type=MESH)

    far_first = sorted(range(1, N), key=lambda j: -min(j, N - j))
    across = y * 4 + (1 - xh) * 2 + core
    for j in far_first:
        greet(r, (c + j) % N)
    greet(across, c)
    for j in range(1, Y):
        greet(row_of((y + j) % Y, core), c)
    greet(mate, c)

    key_rows = pl.ds(pl.multiple_of(share * SH, SH), SH)

    def head(h):
        return pl.ds(pl.multiple_of(h * DH, DH), DH)

    loads = [
        pltpu.make_async_copy(key_blocks_in, key_blocks, in_sem.at[0]),
        pltpu.make_async_copy(query_blocks_in, query_blocks, in_sem.at[1]),
        pltpu.make_async_copy(alpha_in, alpha, in_sem.at[2]),
        pltpu.make_async_copy(tau_in, tau, in_sem.at[3]),
        pltpu.make_async_copy(queries.at[:, head(c)], gq.at[y], in_sem.at[4]),
        pltpu.make_async_copy(out_grad.at[:, head(c)], gg.at[y], in_sem.at[5]),
        pltpu.make_async_copy(keys.at[key_rows, head(c)], gk.at[0, c], in_sem.at[6]),
        pltpu.make_async_copy(values.at[key_rows, head(c)], gv.at[0, c], in_sem.at[7]),
    ]
    for load in loads:
        load.start()
    pl.semaphore_wait(barrier, N + Y)
    pl.semaphore_signal(ready, inc=1, device_id=(across, c), device_id_type=MESH)

    def to_columns(kind):
        for j in far_first:
            peer = (c + j) % N
            src, dst = (
                (keys.at[key_rows, head(peer)], gk.at[0, c]),
                (values.at[key_rows, head(peer)], gv.at[0, c]),
                (gb_send, gb.at[c]),
            )[kind]
            send(src, dst, a_send.at[kind], a_recv.at[kind], r, peer).start()

    own = (queries, out_grad)
    group = (gq, gg)
    HALF = (pl.ds(0, QN // 2), pl.ds(QN // 2, QN // 2))

    def along_y(way, stage):
        step = 1 if way == 0 else 3
        part = HALF[way] if stage != 1 else HALF[1 - way]
        m = y if stage < 2 else (y + 4 - step) % Y
        for kind in (0, 1):
            dst = group[kind].at[m, part]
            src = own[kind].at[part, head(c)] if stage < 2 else dst
            send(
                src, dst, y_send.at[stage // 2], y_recv.at[way, stage], row_of((y + step) % Y, core), c
            ).start()

    def from_y(way, stage):
        landed(y_recv.at[way, stage], gq.at[0])

    to_columns(0)
    for way in (0, 1):
        along_y(way, 0)
    for load in loads[:4]:
        load.wait()
    base = (key_blocks[share // 4] * BLK + (share % 4) * SH).astype(F32)
    gb_send[...] = jnp.full((1, DH), base)
    gb[c] = gb_send[...]
    line = tau[pl.ds(c, 1), :]
    for i in range(4):
        info[y, i : i + 1, :] = line[:, i * DH : (i + 1) * DH]
        info[y, 4 + i : 5 + i, :] = jnp.full((1, DH), query_blocks[i] * BLK).astype(F32)
    to_columns(2)
    for j in range(1, Y):
        send(info.at[y], info.at[y], i_send, i_recv, row_of((y + j) % Y, core), c).start()
    to_columns(1)
    for way in (0, 1):
        along_y(way, 1)

    dk_acc[...] = jnp.zeros_like(dk_acc)
    excess = jnp.full((8, QN), alpha[c]) - 1.0
    scale = excess * FACTOR
    power = (1.0 - excess) / excess * (1.0 / math.log(2.0))
    lane = lax.broadcasted_iota(jnp.int32, (8, QN), 1) % BLK
    row8 = lax.broadcasted_iota(jnp.int32, (8, QN), 0)
    ahead = (lane - row8).astype(F32)

    def wide(tile, lo):
        line = jnp.concatenate([tile[lo + i : lo + i + 1, :] for i in range(4)], axis=1)
        return jnp.broadcast_to(line, (8, QN))

    for load in loads[4:]:
        load.wait()
    for way in (0, 1):
        from_y(way, 0)
        along_y(way, 2)
    landed(i_recv, info.at[0:3])
    landed(a_recv.at[0], gk.at[0, 0 : N - 1])
    to_mate_k = send(gk.at[0], gk.at[1], x_send.at[0], x_recv.at[0], mate, c)
    to_mate_v = send(gv.at[0], gv.at[1], x_send.at[1], x_recv.at[1], mate, c)
    pl.semaphore_wait(ready, 1)
    to_mate_k.start()
    kt[0] = gk[0].reshape(KN, DH).T
    landed(a_recv.at[2], gb.at[0 : N - 1])

    def lines(total):
        total = jnp.sum(total, axis=0, keepdims=True)
        return jnp.concatenate([total[:, i * DH : (i + 1) * DH] for i in range(4)], axis=0)

    def member(t):
        return (y + 4 - place(t)) % Y

    def weigh(h, t):
        m = member(t)
        scores = dot_nt(gk[h].reshape(KN, DH), gq[m])
        tile = info[m]
        shift_in = wide(tile, 0) * excess
        query = wide(tile, 4) + ahead - (h * SH * (other - core)).astype(F32)
        m_sum = jnp.zeros((8, QN), F32)
        for j in range(N):
            b = jnp.broadcast_to(jnp.concatenate([gb[j]] * (QN // DH), axis=1), (8, QN))
            for i in range(SH // 16):
                pair = []
                for lo in (j * SH + i * 16, j * SH + i * 16 + 8):
                    x = scores[lo : lo + 8] * scale - shift_in
                    x = jnp.where(b + (lo - j * SH) <= query, jnp.maximum(x, 0.0), 0.0)
                    w = jnp.exp2(jnp.log(x) * power)
                    w_all[h, t, lo : lo + 8, :] = w
                    pair.append(w * x)
                    m_sum = m_sum + w
                probs[h, t, lo - 8 : lo + 8, :] = jnp.concatenate(pair, axis=0).astype(BF16)
        stats[h, t, 4:8, :] = lines(m_sum)

    def match(h, t):
        dp = dot_nt(gv[h].reshape(KN, DH), gg[member(t)])
        dp_all[h, t] = dp
        t_sum = jnp.zeros((8, QN), F32)
        for lo in range(0, KN, 8):
            t_sum = t_sum + w_all[h, t, lo : lo + 8, :] * dp[lo : lo + 8]
        stats[h, t, 0:4, :] = lines(t_sum)

    def sums_to_y(lo, hi):
        stats[0, lo:hi] = stats[0, lo:hi] + stats[1, lo:hi]
        for j in range(1, Y):
            send(
                stats.at[0, lo:hi], stats_in.at[y, lo:hi], s_send.at[lo // 3], s_recv.at[lo // 3],
                row_of((y + j) % Y, core), c,
            ).start()

    def weigh_and_match(h, t):
        m = member(t)
        scores = dot_nt(gk[h].reshape(KN, DH), gq[m])
        dp = dot_nt(gv[h].reshape(KN, DH), gg[m])
        dp_all[h, t] = dp
        tile = info[m]
        shift_in = wide(tile, 0) * excess
        query = wide(tile, 4) + ahead - (h * SH * (other - core)).astype(F32)
        t_sum = jnp.zeros((8, QN), F32)
        m_sum = jnp.zeros((8, QN), F32)
        for j in range(N):
            b = jnp.broadcast_to(jnp.concatenate([gb[j]] * (QN // DH), axis=1), (8, QN))
            for i in range(SH // 16):
                pair = []
                for lo in (j * SH + i * 16, j * SH + i * 16 + 8):
                    x = scores[lo : lo + 8] * scale - shift_in
                    x = jnp.where(b + (lo - j * SH) <= query, jnp.maximum(x, 0.0), 0.0)
                    w = jnp.exp2(jnp.log(x) * power)
                    w_all[h, t, lo : lo + 8, :] = w
                    pair.append(w * x)
                    t_sum = t_sum + w * dp[lo : lo + 8]
                    m_sum = m_sum + w
                probs[h, t, lo - 8 : lo + 8, :] = jnp.concatenate(pair, axis=0).astype(BF16)
        stats[h, t, 0:4, :] = lines(t_sum)
        stats[h, t, 4:8, :] = lines(m_sum)

    def weigh_early(i, carry):
        for way in (0, 1):

            @pl.when(i == 1 + way)
            def _():
                from_y(way, 1)

        @pl.when(i == 3)
        def _():
            landed(x_recv.at[0], gk.at[1])

        @pl.when(i == 4)
        def _():
            landed(a_recv.at[1], gv.at[0, 0 : N - 1])
            to_mate_v.start()

        weigh(i // 3, i % 3)
        return carry

    def match_own(i, carry):
        match(0, i)
        return carry

    def match_other(i, carry):
        match(1, i)
        return carry

    def rest(i, carry):
        @pl.when(i == 1)
        def _():
            landed(x_recv.at[1], gv.at[1])
            lax.fori_loop(0, 2, match_other, 0)

        weigh_and_match(1 - (2 - i) // 2, 3 - i % 2)

        @pl.when(i == 1)
        def _():
            sums_to_y(0, 3)

        return carry

    lax.fori_loop(0, 5, weigh_early, 0)
    lax.fori_loop(0, 3, match_own, 0)
    for way in (0, 1):
        from_y(way, 2)
    lax.fori_loop(0, 3, rest, 0)
    sums_to_y(3, 4)
    kt[1] = gk[1].reshape(KN, DH).T

    def core_copy(kind):
        return send(core_out.at[kind], core_in.at[kind], c_send.at[kind], c_recv.at[kind], mate, c)

    def add_values(i, carry):
        h = 1 - i // Y
        t = i % Y

        @pl.when(t == 0)
        def _():
            dv_acc[...] = jnp.zeros_like(dv_acc)

        dv_acc[...] += dot(probs[h, t], gg[member(t)])

        @pl.when(i == Y - 1)
        def _():
            core_out[1] = dv_acc[...].astype(BF16)
            core_copy(1).start()

        return carry

    lax.fori_loop(0, 2 * Y, add_values, 0, unroll=2)

    def send_last(kind, total):
        landed(c_recv.at[kind], core_in.at[kind])
        total = total + core_in[kind].astype(F32)
        own_part[kind] = total.astype(BF16).reshape(N, SH, DH)

        def one(j):
            peer = (c + j) % N
            send(
                own_part.at[kind, peer], row_part.at[kind, r], p_send.at[kind], p_recv.at[kind], c, peer
            ).start()

        for j in far_first:
            one(j)

        @pl.when(c != r)
        def _():
            one(0)

        @pl.when(c == r)
        def _():
            row_part[kind, r] = own_part[kind, c]

    def finish(kind, out, factor):
        @pl.when(c != r)
        def _():
            landed(p_recv.at[kind], row_part.at[kind])

        @pl.when(c == r)
        def _():
            landed(p_recv.at[kind], row_part.at[kind, 0 : N - 1])

        pairs = row_part[kind].astype(F32).reshape(4, 2, 2, SH, DH)
        pairs = (pairs[:, 0] + pairs[:, 1]).reshape(8 * SH, DH)
        out[...] = (pairs.T * factor).astype(BF16)

    landed(s_recv.at[0], stats_in.at[0:3, 0:3])
    landed(s_recv.at[1], stats_in.at[0:3, 3:4])
    stats_in[y] = stats[0]

    def one_shift(t, carry):
        m = member(t)
        total = jnp.zeros((8, DH), F32)
        for src in range(Y):
            total = total + stats_in[src, place((src + 4 - m) % Y)]
        shift = total[0:4] / jnp.maximum(total[4:8], 1.0)
        shifts[t] = wide(shift, 0)
        return carry

    lax.fori_loop(0, Y, one_shift, 0)

    def score_grad(h, t):
        row_shift = shifts[t]
        for lo in range(0, KN, 16):
            pair = [w_all[h, t, i : i + 8, :] * (dp_all[h, t, i : i + 8, :] - row_shift) for i in (lo, lo + 8)]
            probs[h, t, lo : lo + 16, :] = jnp.concatenate(pair, axis=0).astype(BF16)
        ds = probs[h, t]
        dk_acc[h] += dot(ds, gq[member(t)])
        return ds

    def other_share(i, carry):
        score_grad(1, 3 - i)
        return carry

    def own_share(i, carry):
        t = 3 - i
        ds = score_grad(0, t)
        part = dot(kt[0], ds) + dot(kt[1], probs[1, t])

        @pl.when(t == 0)
        def _():
            dq_own[...] = part

        @pl.when(t > 0)
        def _():
            dq_send[t] = part.astype(BF16)

        for tt in (3, 2, 1):

            @pl.when(t == tt)
            def _():
                send(dq_send.at[tt], dq_in.at[tt - 1], d_send, d_recv, row_of(member(tt), core), c).start()

        @pl.when(i == 1)
        def _():
            send_last(1, dv_acc[...])

        return carry

    lax.fori_loop(0, Y, other_share, 0, unroll=2)
    core_out[0] = dk_acc[1].astype(BF16)
    core_copy(0).start()
    lax.fori_loop(0, Y, own_share, 0, unroll=2)
    send_last(0, dk_acc[0])
    finish(1, dv_out, 1.0)
    landed(d_recv, dq_in)
    dq = dq_own[...]
    for t in range(3):
        dq = dq + dq_in[t].astype(F32)
    dq_out[...] = (dq * FACTOR).astype(BF16)
    finish(0, dk_out, FACTOR)

    left(a_send.at[0], gk.at[0, 0 : N - 1])
    left(a_send.at[1], gv.at[0, 0 : N - 1])
    left(a_send.at[2], gb.at[0 : N - 1])
    left(i_send, info.at[0:3])
    left(y_send.at[0], gq)
    left(y_send.at[1], gq.at[0:2])
    to_mate_k.wait_send()
    to_mate_v.wait_send()
    left(s_send.at[0], stats_in.at[0:3, 0:3])
    left(s_send.at[1], stats_in.at[0:3, 3:4])
    left(d_send, dq_in)
    for kind in (0, 1):
        core_copy(kind).wait_send()

        @pl.when(c != r)
        def _():
            left(p_send.at[kind], own_part.at[kind])

        @pl.when(c == r)
        def _():
            left(p_send.at[kind], own_part.at[kind, 0 : N - 1])


def store(dq, dk, dv, dq_out, dk_out, dv_out, sem):
    copies = [
        pltpu.make_async_copy(src, dst, sem.at[i])
        for i, (src, dst) in enumerate(((dq, dq_out), (dk, dk_out), (dv, dv_out)))
    ]
    for copy in copies:
        copy.start()
    for copy in copies:
        copy.wait()


def local(*args):
    hbm = pl.BlockSpec(memory_space=pltpu.HBM)
    vmem = pl.BlockSpec(memory_space=pltpu.VMEM)
    V = pltpu.VMEM
    S = pltpu.SMEM
    dma = pltpu.SemaphoreType.DMA
    one = pltpu.SemaphoreType.DMA(())
    shapes = (
        jax.ShapeDtypeStruct((DH, QN), BF16),
        jax.ShapeDtypeStruct((DH, 2 * BLK), BF16),
        jax.ShapeDtypeStruct((DH, 2 * BLK), BF16),
    )
    grads = pl.pallas_call(
        kernel,
        out_shape=shapes,
        in_specs=[hbm] * 8,
        out_specs=(vmem,) * 3,
        scratch_shapes=[
            S((N,), F32), S((4,), jnp.int32), S((2,), jnp.int32), V((N, QN), F32),
            V((2, N, SH, DH), BF16), V((2, N, SH, DH), BF16), V((N, 1, DH), F32), V((1, DH), F32),
            V((Y, QN, DH), BF16), V((Y, QN, DH), BF16), V((Y, 8, DH), F32),
            V((2, DH, KN), BF16), V((2, Y, KN, QN), F32), V((2, Y, KN, QN), F32), V((2, Y, KN, QN), BF16),
            V((KN, DH), F32), V((2, KN, DH), F32), V((DH, QN), F32), V((2, Y, 8, DH), F32), V((Y, Y, 8, DH), F32), V((Y, 8, QN), F32),
            V((2, KN, DH), BF16), V((2, KN, DH), BF16), V((Y, DH, QN), BF16), V((3, DH, QN), BF16),
            V((2, N, SH, DH), BF16), V((2, N, SH, DH), BF16),
            dma((8,)), dma((3,)), dma((3,)), dma((2,)), dma((2,)), dma((2,)), dma((2, 3)), one, one, dma((2,)), dma((2,)),
            dma((2,)), dma((2,)), one, one, dma((2,)), dma((2,)), pltpu.SemaphoreType.REGULAR,
        ],
        compiler_params=pltpu.CompilerParams(
            collective_id=0, has_side_effects=True, vmem_limit_bytes=48 * 1024 * 1024
        ),
    )(*[pltpu.with_memory_space_constraint(a, pltpu.HBM) for a in args])

    return pl.pallas_call(
        store,
        out_shape=shapes,
        in_specs=[vmem] * 3,
        out_specs=(hbm,) * 3,
        scratch_shapes=[dma((3,))],
    )(*[pltpu.with_memory_space_constraint(g, pltpu.VMEM) for g in grads])

def solution(mesh):
    in_specs = (
        P("row", None), P("col", None), P("col", None), P("row", None),
        P(None, "row"), P(), P("row"), P("col"),
    )
    out_specs = (P("col", "row"), P("row", "col"), P("row", "col"))
    return jax.shard_map(local, mesh=mesh, in_specs=in_specs, out_specs=out_specs, check_vma=False)
```

```python
import math

import jax
import jax.numpy as jnp
from jax import lax
from jax.experimental import pallas as pl
from jax.experimental.pallas import tpu as pltpu
from jax.sharding import PartitionSpec as P

MESH = pl.DeviceIdType.MESH
DH = 128
BLK = 128
QN = 512
N = 16
SH = 32
KN = N * SH
Y = 4
F32 = jnp.float32
BF16 = jnp.bfloat16
FACTOR = 1.0 / math.sqrt(DH)


def dot(a, b):
    return jnp.dot(a, b, preferred_element_type=F32)


def dot_nt(a, b):
    return lax.dot_general(a, b, (((1,), (1,)), ((), ())), preferred_element_type=F32)


def place(t):
    return t + t // 2 - 2 * (t // 3)


def kernel(
    queries, keys, values, out_grad, tau_in, alpha_in, query_blocks_in, key_blocks_in,
    dq_out, dk_out, dv_out,
    alpha, query_blocks, key_blocks, tau,
    gk, gv, gb, gb_send,
    gq, gg, info,
    kt, w_all, dp_all, probs, dv_acc, dk_acc, stats, stats_in, shifts,
    core_out, core_in, dq_send, dq_in, own_part, row_part,
    in_sem, a_send, a_recv, x_send, x_recv, y_send, y_recv, i_send, i_recv, s_send, s_recv,
    c_send, c_recv, d_send, d_recv, p_send, p_recv, ready,
):
    r = lax.axis_index("row")
    c = lax.axis_index("col")
    y = r // 4
    xh = (r // 2) % 2
    core = r % 2
    other = 1 - core
    share = y * 2 + core

    def row_of(yy, cc):
        return yy * 4 + xh * 2 + cc

    mate = row_of(y, other)

    def send(src, dst, ssem, rsem, row, col):
        return pltpu.make_async_remote_copy(
            src_ref=src, dst_ref=dst, send_sem=ssem, recv_sem=rsem,
            device_id=(row, col), device_id_type=MESH,
        )

    def landed(sem, ref):
        send(ref, ref, in_sem.at[0], sem, mate, c).wait_recv()

    def left(sem, ref):
        send(ref, ref, sem, in_sem.at[0], mate, c).wait_send()

    barrier = pltpu.get_barrier_semaphore()

    def greet(row, col):
        pl.semaphore_signal(barrier, inc=1, device_id=(row, col), device_id_type=MESH)

    far_first = sorted(range(1, N), key=lambda j: -min(j, N - j))
    across = y * 4 + (1 - xh) * 2 + core
    for j in far_first:
        greet(r, (c + j) % N)
    greet(across, c)
    for j in range(1, Y):
        greet(row_of((y + j) % Y, core), c)
    greet(mate, c)

    key_rows = pl.ds(pl.multiple_of(share * SH, SH), SH)

    def head(h):
        return pl.ds(pl.multiple_of(h * DH, DH), DH)

    loads = [
        pltpu.make_async_copy(key_blocks_in, key_blocks, in_sem.at[0]),
        pltpu.make_async_copy(query_blocks_in, query_blocks, in_sem.at[1]),
        pltpu.make_async_copy(alpha_in, alpha, in_sem.at[2]),
        pltpu.make_async_copy(tau_in, tau, in_sem.at[3]),
        pltpu.make_async_copy(queries.at[:, head(c)], gq.at[y], in_sem.at[4]),
        pltpu.make_async_copy(out_grad.at[:, head(c)], gg.at[y], in_sem.at[5]),
        pltpu.make_async_copy(keys.at[key_rows, head(c)], gk.at[0, c], in_sem.at[6]),
        pltpu.make_async_copy(values.at[key_rows, head(c)], gv.at[0, c], in_sem.at[7]),
    ]
    for load in loads:
        load.start()
    pl.semaphore_wait(barrier, N + Y)
    pl.semaphore_signal(ready, inc=1, device_id=(across, c), device_id_type=MESH)

    def to_columns(kind):
        for j in far_first:
            peer = (c + j) % N
            src, dst = (
                (keys.at[key_rows, head(peer)], gk.at[0, c]),
                (values.at[key_rows, head(peer)], gv.at[0, c]),
                (gb_send, gb.at[c]),
            )[kind]
            send(src, dst, a_send.at[kind], a_recv.at[kind], r, peer).start()

    own = (queries, out_grad)
    group = (gq, gg)
    HALF = (pl.ds(0, QN // 2), pl.ds(QN // 2, QN // 2))

    def along_y(way, stage):
        step = 1 if way == 0 else 3
        part = HALF[way] if stage != 1 else HALF[1 - way]
        m = y if stage < 2 else (y + 4 - step) % Y
        for kind in (0, 1):
            dst = group[kind].at[m, part]
            src = own[kind].at[part, head(c)] if stage < 2 else dst
            send(
                src, dst, y_send.at[stage // 2], y_recv.at[way, stage], row_of((y + step) % Y, core), c
            ).start()

    def from_y(way, stage):
        landed(y_recv.at[way, stage], gq.at[0])

    to_columns(0)
    for way in (0, 1):
        along_y(way, 0)
    for load in loads[:4]:
        load.wait()
    base = (key_blocks[share // 4] * BLK + (share % 4) * SH).astype(F32)
    gb_send[...] = jnp.full((1, DH), base)
    gb[c] = gb_send[...]
    line = tau[pl.ds(c, 1), :]
    for i in range(4):
        info[y, i : i + 1, :] = line[:, i * DH : (i + 1) * DH]
        info[y, 4 + i : 5 + i, :] = jnp.full((1, DH), query_blocks[i] * BLK).astype(F32)
    to_columns(2)
    for j in range(1, Y):
        send(info.at[y], info.at[y], i_send, i_recv, row_of((y + j) % Y, core), c).start()
    to_columns(1)
    for way in (0, 1):
        along_y(way, 1)

    dk_acc[...] = jnp.zeros_like(dk_acc)
    excess = jnp.full((8, QN), alpha[c]) - 1.0
    scale = excess * FACTOR
    power = (1.0 - excess) / excess * (1.0 / math.log(2.0))
    lane = lax.broadcasted_iota(jnp.int32, (8, QN), 1) % BLK
    row8 = lax.broadcasted_iota(jnp.int32, (8, QN), 0)
    ahead = (lane - row8).astype(F32)

    def wide(tile, lo):
        line = jnp.concatenate([tile[lo + i : lo + i + 1, :] for i in range(4)], axis=1)
        return jnp.broadcast_to(line, (8, QN))

    for load in loads[4:]:
        load.wait()
    for way in (0, 1):
        from_y(way, 0)
        along_y(way, 2)
    landed(i_recv, info.at[0:3])
    landed(a_recv.at[0], gk.at[0, 0 : N - 1])
    to_mate_k = send(gk.at[0], gk.at[1], x_send.at[0], x_recv.at[0], mate, c)
    to_mate_v = send(gv.at[0], gv.at[1], x_send.at[1], x_recv.at[1], mate, c)
    pl.semaphore_wait(ready, 1)
    to_mate_k.start()
    kt[0] = gk[0].reshape(KN, DH).T
    landed(a_recv.at[2], gb.at[0 : N - 1])

    def lines(total):
        total = jnp.sum(total, axis=0, keepdims=True)
        return jnp.concatenate([total[:, i * DH : (i + 1) * DH] for i in range(4)], axis=0)

    def member(t):
        return (y + 4 - place(t)) % Y

    def weigh(h, t):
        m = member(t)
        scores = dot_nt(gk[h].reshape(KN, DH), gq[m])
        tile = info[m]
        shift_in = wide(tile, 0) * excess
        query = wide(tile, 4) + ahead - (h * SH * (other - core)).astype(F32)
        m_sum = jnp.zeros((8, QN), F32)
        for j in range(N):
            b = jnp.broadcast_to(jnp.concatenate([gb[j]] * (QN // DH), axis=1), (8, QN))
            for i in range(SH // 16):
                pair = []
                for lo in (j * SH + i * 16, j * SH + i * 16 + 8):
                    x = scores[lo : lo + 8] * scale - shift_in
                    x = jnp.where(b + (lo - j * SH) <= query, jnp.maximum(x, 0.0), 0.0)
                    w = jnp.exp2(jnp.log(x) * power)
                    w_all[h, t, lo : lo + 8, :] = w
                    pair.append(w * x)
                    m_sum = m_sum + w
                probs[h, t, lo - 8 : lo + 8, :] = jnp.concatenate(pair, axis=0).astype(BF16)
        stats[h, t, 4:8, :] = lines(m_sum)

    def match(h, t):
        dp = dot_nt(gv[h].reshape(KN, DH), gg[member(t)])
        dp_all[h, t] = dp
        t_sum = jnp.zeros((8, QN), F32)
        for lo in range(0, KN, 8):
            t_sum = t_sum + w_all[h, t, lo : lo + 8, :] * dp[lo : lo + 8]
        stats[h, t, 0:4, :] = lines(t_sum)

    def sums_to_y(lo, hi):
        stats[0, lo:hi] = stats[0, lo:hi] + stats[1, lo:hi]
        for j in range(1, Y):
            send(
                stats.at[0, lo:hi], stats_in.at[y, lo:hi], s_send.at[lo // 3], s_recv.at[lo // 3],
                row_of((y + j) % Y, core), c,
            ).start()

    def weigh_and_match(h, t):
        m = member(t)
        scores = dot_nt(gk[h].reshape(KN, DH), gq[m])
        dp = dot_nt(gv[h].reshape(KN, DH), gg[m])
        dp_all[h, t] = dp
        tile = info[m]
        shift_in = wide(tile, 0) * excess
        query = wide(tile, 4) + ahead - (h * SH * (other - core)).astype(F32)
        t_sum = jnp.zeros((8, QN), F32)
        m_sum = jnp.zeros((8, QN), F32)
        for j in range(N):
            b = jnp.broadcast_to(jnp.concatenate([gb[j]] * (QN // DH), axis=1), (8, QN))
            for i in range(SH // 16):
                pair = []
                for lo in (j * SH + i * 16, j * SH + i * 16 + 8):
                    x = scores[lo : lo + 8] * scale - shift_in
                    x = jnp.where(b + (lo - j * SH) <= query, jnp.maximum(x, 0.0), 0.0)
                    w = jnp.exp2(jnp.log(x) * power)
                    w_all[h, t, lo : lo + 8, :] = w
                    pair.append(w * x)
                    t_sum = t_sum + w * dp[lo : lo + 8]
                    m_sum = m_sum + w
                probs[h, t, lo - 8 : lo + 8, :] = jnp.concatenate(pair, axis=0).astype(BF16)
        stats[h, t, 0:4, :] = lines(t_sum)
        stats[h, t, 4:8, :] = lines(m_sum)

    def weigh_early(i, carry):
        for way in (0, 1):

            @pl.when(i == 1 + way)
            def _():
                from_y(way, 1)

        @pl.when(i == 3)
        def _():
            landed(x_recv.at[0], gk.at[1])

        @pl.when(i == 4)
        def _():
            landed(a_recv.at[1], gv.at[0, 0 : N - 1])
            to_mate_v.start()

        weigh(i // 3, i % 3)
        return carry

    def match_own(i, carry):
        match(0, i)
        return carry

    def match_other(i, carry):
        match(1, i)
        return carry

    def rest(i, carry):
        @pl.when(i == 1)
        def _():
            landed(x_recv.at[1], gv.at[1])
            lax.fori_loop(0, 2, match_other, 0)

        weigh_and_match(1 - (2 - i) // 2, 3 - i % 2)

        @pl.when(i == 1)
        def _():
            sums_to_y(0, 3)

        return carry

    lax.fori_loop(0, 5, weigh_early, 0)
    lax.fori_loop(0, 3, match_own, 0)
    for way in (0, 1):
        from_y(way, 2)
    lax.fori_loop(0, 3, rest, 0)
    sums_to_y(3, 4)
    kt[1] = gk[1].reshape(KN, DH).T

    def core_copy(kind):
        return send(core_out.at[kind], core_in.at[kind], c_send.at[kind], c_recv.at[kind], mate, c)

    def add_values(i, carry):
        h = 1 - i // Y
        t = i % Y

        @pl.when(t == 0)
        def _():
            dv_acc[...] = jnp.zeros_like(dv_acc)

        dv_acc[...] += dot(probs[h, t], gg[member(t)])

        @pl.when(i == Y - 1)
        def _():
            core_out[1] = dv_acc[...].astype(BF16)
            core_copy(1).start()

        return carry

    lax.fori_loop(0, 2 * Y, add_values, 0, unroll=2)

    def send_last(kind, total):
        landed(c_recv.at[kind], core_in.at[kind])
        total = total + core_in[kind].astype(F32)
        own_part[kind] = total.astype(BF16).reshape(N, SH, DH)

        def one(j):
            peer = (c + j) % N
            send(
                own_part.at[kind, peer], row_part.at[kind, r], p_send.at[kind], p_recv.at[kind], c, peer
            ).start()

        for j in far_first:
            one(j)

        @pl.when(c != r)
        def _():
            one(0)

        @pl.when(c == r)
        def _():
            row_part[kind, r] = own_part[kind, c]

    def finish(kind, out, factor):
        @pl.when(c != r)
        def _():
            landed(p_recv.at[kind], row_part.at[kind])

        @pl.when(c == r)
        def _():
            landed(p_recv.at[kind], row_part.at[kind, 0 : N - 1])

        pairs = row_part[kind].astype(F32).reshape(4, 2, 2, SH, DH)
        pairs = (pairs[:, 0] + pairs[:, 1]).reshape(8 * SH, DH)
        out[...] = (pairs.T * factor).astype(BF16)

    landed(s_recv.at[0], stats_in.at[0:3, 0:3])
    landed(s_recv.at[1], stats_in.at[0:3, 3:4])
    stats_in[y] = stats[0]

    def one_shift(t, carry):
        m = member(t)
        total = jnp.zeros((8, DH), F32)
        for src in range(Y):
            total = total + stats_in[src, place((src + 4 - m) % Y)]
        shift = total[0:4] / jnp.maximum(total[4:8], 1.0)
        shifts[t] = wide(shift, 0)
        return carry

    lax.fori_loop(0, Y, one_shift, 0)

    def score_grad(h, t):
        row_shift = shifts[t]
        for lo in range(0, KN, 16):
            pair = [w_all[h, t, i : i + 8, :] * (dp_all[h, t, i : i + 8, :] - row_shift) for i in (lo, lo + 8)]
            probs[h, t, lo : lo + 16, :] = jnp.concatenate(pair, axis=0).astype(BF16)
        ds = probs[h, t]
        dk_acc[h] += dot(ds, gq[member(t)])
        return ds

    def other_share(i, carry):
        score_grad(1, 3 - i)
        return carry

    def own_share(i, carry):
        t = 3 - i
        ds = score_grad(0, t)
        @pl.when(t > 0)
        def _():
            dq_send[t] = (dot(kt[0], ds) + dot(kt[1], probs[1, t])).astype(BF16)

        for tt in (3, 2, 1):

            @pl.when(t == tt)
            def _():
                send(dq_send.at[tt], dq_in.at[tt - 1], d_send, d_recv, row_of(member(tt), core), c).start()

        @pl.when(i == 1)
        def _():
            send_last(1, dv_acc[...])

        return carry

    lax.fori_loop(0, Y, other_share, 0, unroll=2)
    core_out[0] = dk_acc[1].astype(BF16)
    core_copy(0).start()
    lax.fori_loop(0, Y, own_share, 0, unroll=2)
    send_last(0, dk_acc[0])
    dq = dot(kt[0], probs[0, 0]) + dot(kt[1], probs[1, 0])
    finish(1, dv_out, 1.0)
    landed(d_recv, dq_in)
    for t in range(3):
        dq = dq + dq_in[t].astype(F32)
    dq_out[...] = (dq * FACTOR).astype(BF16)
    finish(0, dk_out, FACTOR)

    left(a_send.at[0], gk.at[0, 0 : N - 1])
    left(a_send.at[1], gv.at[0, 0 : N - 1])
    left(a_send.at[2], gb.at[0 : N - 1])
    left(i_send, info.at[0:3])
    left(y_send.at[0], gq)
    left(y_send.at[1], gq.at[0:2])
    to_mate_k.wait_send()
    to_mate_v.wait_send()
    left(s_send.at[0], stats_in.at[0:3, 0:3])
    left(s_send.at[1], stats_in.at[0:3, 3:4])
    left(d_send, dq_in)
    for kind in (0, 1):
        core_copy(kind).wait_send()

        @pl.when(c != r)
        def _():
            left(p_send.at[kind], own_part.at[kind])

        @pl.when(c == r)
        def _():
            left(p_send.at[kind], own_part.at[kind, 0 : N - 1])


def store(dq, dk, dv, dq_out, dk_out, dv_out, sem):
    copies = [
        pltpu.make_async_copy(src, dst, sem.at[i])
        for i, (src, dst) in enumerate(((dq, dq_out), (dk, dk_out), (dv, dv_out)))
    ]
    for copy in copies:
        copy.start()
    for copy in copies:
        copy.wait()


def local(*args):
    hbm = pl.BlockSpec(memory_space=pltpu.HBM)
    vmem = pl.BlockSpec(memory_space=pltpu.VMEM)
    V = pltpu.VMEM
    S = pltpu.SMEM
    dma = pltpu.SemaphoreType.DMA
    one = pltpu.SemaphoreType.DMA(())
    shapes = (
        jax.ShapeDtypeStruct((DH, QN), BF16),
        jax.ShapeDtypeStruct((DH, 2 * BLK), BF16),
        jax.ShapeDtypeStruct((DH, 2 * BLK), BF16),
    )
    grads = pl.pallas_call(
        kernel,
        out_shape=shapes,
        in_specs=[hbm] * 8,
        out_specs=(vmem,) * 3,
        scratch_shapes=[
            S((N,), F32), S((4,), jnp.int32), S((2,), jnp.int32), V((N, QN), F32),
            V((2, N, SH, DH), BF16), V((2, N, SH, DH), BF16), V((N, 1, DH), F32), V((1, DH), F32),
            V((Y, QN, DH), BF16), V((Y, QN, DH), BF16), V((Y, 8, DH), F32),
            V((2, DH, KN), BF16), V((2, Y, KN, QN), F32), V((2, Y, KN, QN), F32), V((2, Y, KN, QN), BF16),
            V((KN, DH), F32), V((2, KN, DH), F32), V((2, Y, 8, DH), F32), V((Y, Y, 8, DH), F32), V((Y, 8, QN), F32),
            V((2, KN, DH), BF16), V((2, KN, DH), BF16), V((Y, DH, QN), BF16), V((3, DH, QN), BF16),
            V((2, N, SH, DH), BF16), V((2, N, SH, DH), BF16),
            dma((8,)), dma((3,)), dma((3,)), dma((2,)), dma((2,)), dma((2,)), dma((2, 3)), one, one, dma((2,)), dma((2,)),
            dma((2,)), dma((2,)), one, one, dma((2,)), dma((2,)), pltpu.SemaphoreType.REGULAR,
        ],
        compiler_params=pltpu.CompilerParams(
            collective_id=0, has_side_effects=True, vmem_limit_bytes=48 * 1024 * 1024
        ),
    )(*[pltpu.with_memory_space_constraint(a, pltpu.HBM) for a in args])

    return pl.pallas_call(
        store,
        out_shape=shapes,
        in_specs=[vmem] * 3,
        out_specs=(hbm,) * 3,
        scratch_shapes=[dma((3,))],
    )(*[pltpu.with_memory_space_constraint(g, pltpu.VMEM) for g in grads])

def solution(mesh):
    in_specs = (
        P("row", None), P("col", None), P("col", None), P("row", None),
        P(None, "row"), P(), P("row"), P("col"),
    )
    out_specs = (P("col", "row"), P("row", "col"), P("row", "col"))
    return jax.shard_map(local, mesh=mesh, in_specs=in_specs, out_specs=out_specs, check_vma=False)
```
